128 devices in a mesh: sample: 8 (over z, core), space: 16 (over y, x).
Axes of the slice: x: 4, y: 4, z: 4, core: 2. Of those that a mesh axis runs over, the one named last changes fastest.
Arguments:
- displacements: bfloat16 [64, 3, 296208], P('sample', None, 'space')
- connectivity: int32 [8, 262144], P(None, 'space'), may hold values from 0 to 18512, as said below
- density: float32 [262144], P('space'), may hold values from 0.1 to 1
- stiffness: bfloat16 [24, 24], replicated
- filter_inverse: float32 [128, 128], replicated
- send_rows: int32 [16, 8, 16, 256], P('space'), may hold values from 0 to 2047, as said below
- send_count: int32 [16, 8, 16], P('space'), may hold values from 0 to 256, as said below
- recv_cell: int32 [8, 16, 16, 256], P('sample', 'space'), may hold values from 0 to 2047
Outputs:
- compliance: float32 [64], replicated
- filtered_sensitivity: float32 [8, 16, 2048], P('sample', 'space')
- filtered_energy: float32 [8, 16, 2048], P('sample', 'space')
The draws below stay inside these ranges and needn't reach their ends.
Inputs may be any that keep to these rules, and one draw needn't show every extreme that they name: `connectivity`: column j * 16384 + e lists the eight distinct corner nodes of element e of slab j, as indices into that slab's 18513 nodes. `send_rows`: for each slab j and group i, the first send_count[j, i, d] slots of the lists over all d hold each of the group's 2048 elements exactly once; other slots hold 0. `send_count`: for each slab and group the counts over destinations sum to 2048, and one destination takes exactly 256.
All inputs are finite; a program needn't handle non-finite values.
Results may differ from the reference program's by a relative error of at most 0.0003.
Values sent between devices are 32-bit elements; how exact they have to be, the bound alone decides.
No kernel may reach another device: no remote copies, remote signals or barrier semaphores. Data moves between devices by JAX's collectives and lax.ppermute only.
A program may use at most 128 MiB of HBM per device.

```python
import jax
import jax.numpy as jnp
import numpy as np
from jax import lax

CX = 32
CY = 32
CZ = 16
SAMPLES = 64
PATCH = 128
E_DEV = 16384
NODES_DEV = 18513
SLABS = 16
GROUPS = 8
ELEMS = 262144
NODES = 296208
EB = 2048
CAP = 256


def draw_displacements(key, part):
    base_key = jax.random.fold_in(key, 11)
    key_wave, key_amp, key_phase, key_noise, key_sample = jax.random.split(base_key, 5)
    node_ids = jnp.arange(NODES, dtype=jnp.int32)
    slab_ids = (node_ids // NODES_DEV).astype(jnp.float32)
    local_ids = node_ids % NODES_DEV
    x_layer = (local_ids // ((CY + 1) * (CZ + 1))).astype(jnp.float32)
    y_layer = (local_ids // (CZ + 1) % (CY + 1)).astype(jnp.float32)
    z_layer = (local_ids % (CZ + 1)).astype(jnp.float32)
    x_coord = slab_ids + x_layer / CX
    y_coord = y_layer / CY
    z_coord = z_layer / CZ
    waves = jax.random.uniform(key_wave, (4, 3), jnp.float32, 0.5, 3.0)
    amplitude = jax.random.normal(key_amp, (SAMPLES, 3, 4), jnp.float32)
    phases = jax.random.uniform(key_phase, (SAMPLES, 3, 4), jnp.float32, -3.14159, 3.14159)
    shape = (SAMPLES, 3, NODES)
    noise = jax.random.normal(key_noise, shape, jnp.float32)
    sample_scale = jnp.exp(jax.random.uniform(key_sample, (SAMPLES,), jnp.float32, -0.7, 0.7))
    smooth_field = jnp.zeros(shape, jnp.float32)
    for mode in range(4):
        argument = waves[mode, 0] * x_coord + waves[mode, 1] * y_coord + waves[mode, 2] * z_coord
        smooth_field = smooth_field + amplitude[:, :, mode, None] * jnp.cos(argument[None, None, :] + phases[:, :, mode, None])
    position = (0.5 + slab_ids / (SLABS - 1)) * (0.6 + 0.8 * x_layer / CX)
    values = (0.06 * smooth_field + 0.02 * noise) * sample_scale[:, None, None] * position[None, None, :]
    return values.astype(jnp.bfloat16)


def draw_connectivity(key, part):
    corner_x = jnp.array(np.array([0, 1, 1, 0, 0, 1, 1, 0]), jnp.int32)[:, None]
    corner_y = jnp.array(np.array([0, 0, 1, 1, 0, 0, 1, 1]), jnp.int32)[:, None]
    corner_z = jnp.array(np.array([0, 0, 0, 0, 1, 1, 1, 1]), jnp.int32)[:, None]

    def one_slab(slab_id):
        element_order = jax.random.permutation(jax.random.fold_in(jax.random.fold_in(key, 77), slab_id), E_DEV).astype(jnp.int32)
        along_x = element_order // (CY * CZ)
        along_y = element_order // CZ % CY
        along_z = element_order % CZ
        return ((along_x[None, :] + corner_x) * (CY + 1) + (along_y[None, :] + corner_y)) * (CZ + 1) + (along_z[None, :] + corner_z)
    blocks = jax.vmap(one_slab)(jnp.arange(SLABS, dtype=jnp.int32))
    return jnp.transpose(blocks, (1, 0, 2)).reshape(8, ELEMS).astype(jnp.int32)


def draw_stiffness(key, part):
    key_same, key_cross, key_diag = jax.random.split(jax.random.fold_in(key, 23), 3)
    raw_same = jax.random.uniform(key_same, (24, 24), jnp.float32, 0.2, 1.0)
    raw_cross = jax.random.uniform(key_cross, (24, 24), jnp.float32, -0.2, 0.2)
    same_part = -(raw_same + raw_same.T) * 0.5
    cross_part = (raw_cross + raw_cross.T) * 0.5
    index_ids = jnp.arange(24, dtype=jnp.int32)
    component = index_ids // 8
    same_comp = component[:, None] == component[None, :]
    off_part = jnp.where(same_comp, same_part, cross_part)
    diag_part = 10.5 + jax.random.uniform(key_diag, (24,), jnp.float32, 0.0, 1.0)
    on_diag = index_ids[:, None] == index_ids[None, :]
    return jnp.where(on_diag, diag_part[None, :] * jnp.ones((24, 24), jnp.float32), off_part).astype(jnp.bfloat16)


def draw_filter_inverse(key, part):
    index_ids = jnp.arange(PATCH, dtype=jnp.int32)
    distance = jnp.abs(index_ids[:, None] - index_ids[None, :]).astype(jnp.float32)
    decay = jnp.exp(-distance / (PATCH / 4.0))
    factor = jax.random.uniform(jax.random.fold_in(key, 31), (PATCH, PATCH), jnp.float32, 0.6, 1.4)
    return (factor * decay * (4.0 / PATCH)).astype(jnp.float32)


def list_plan(key):
    base_key = jax.random.fold_in(key, 4242)
    middle = EB // SLABS

    def one_list(list_id):
        key_order, key_shift, key_perm = jax.random.split(jax.random.fold_in(base_key, list_id), 3)
        dest_order = jax.random.permutation(key_order, SLABS).astype(jnp.int32)
        shifts = jax.random.randint(key_shift, (SLABS // 2 - 1,), 0, middle, dtype=jnp.int32)
        paired = jnp.stack([middle + shifts, middle - shifts], axis=1).reshape(-1)
        values = jnp.concatenate([jnp.array([2 * middle, 0], jnp.int32), paired])
        counts = jnp.zeros((SLABS,), jnp.int32).at[dest_order].set(values)
        element_perm = jax.random.permutation(key_perm, EB).astype(jnp.int32)
        offsets = jnp.cumsum(counts) - counts
        slot_ids = jnp.arange(CAP, dtype=jnp.int32)
        pick_ids = jnp.minimum(offsets[:, None] + slot_ids[None, :], EB - 1)
        listed = jnp.where(slot_ids[None, :] < counts[:, None], element_perm[pick_ids], 0)
        return (listed.astype(jnp.int32), counts)
    listed, counts = jax.vmap(one_list)(jnp.arange(SLABS * GROUPS, dtype=jnp.int32))
    return (listed.reshape(SLABS, GROUPS, SLABS, CAP), counts.reshape(SLABS, GROUPS, SLABS))


def draw_send_rows(key, part):
    return list_plan(key)[0]


def draw_send_count(key, part):
    return list_plan(key)[1]


def touch_ends(drawn, rng, least, high):
    dims = drawn.shape
    spot = [jax.random.randint(jax.random.fold_in(rng, axis), (), 0, dims[axis]) for axis in range(len(dims))]
    drawn = drawn.at[tuple(spot)].set(least)
    longest = dims.index(max(dims))
    spot[longest] = (spot[longest] + 1) % dims[longest]
    return drawn.at[tuple(spot)].set(high)


def level_of(stream_key, extent, pieces, least, high):
    gain, own = 1.0, jax.random.fold_in(stream_key, 6)
    for dim, blocks in pieces:
        steps = jnp.exp(jax.random.uniform(jax.random.fold_in(own, dim), (blocks,), jnp.float32, least / len(pieces), high / len(pieces)))
        gain = gain * jnp.repeat(steps, extent[dim] // blocks).reshape([-1 if axis == dim else 1 for axis in range(len(extent))])
    return gain


def setup_inputs(seed: int = 0) -> dict:
    key_of = jax.random.split(jax.random.key(seed), 9)
    return {
        "displacements": draw_displacements(jax.random.fold_in(key_of[8], 71), 0),
        "connectivity": draw_connectivity(jax.random.fold_in(key_of[8], 71), 0),
        "density": jnp.clip(0.1 + 0.9 * jax.random.uniform(key_of[2], (ELEMS,), jnp.float32) ** level_of(key_of[2], (ELEMS,), ((0, 16),), -0.2, 0.2), 0.1, 1.0),
        "stiffness": draw_stiffness(jax.random.fold_in(key_of[8], 71), 0),
        "filter_inverse": draw_filter_inverse(jax.random.fold_in(key_of[8], 71), 0),
        "send_rows": draw_send_rows(jax.random.fold_in(key_of[8], 71), 0),
        "send_count": draw_send_count(jax.random.fold_in(key_of[8], 71), 0),
        "recv_cell": touch_ends(jax.random.randint(key_of[7], (GROUPS, SLABS, SLABS, CAP), 0, EB), jax.random.fold_in(key_of[7], 1), 0, EB - 1).astype(jnp.int32),
    }


penalty = 3.0
spread_weight = 0.5
epsilon = 1e-06

def robust_weights(compliance):
    center = jnp.mean(compliance)
    spread = jnp.sqrt(jnp.mean((compliance - center) ** 2) + epsilon)
    return (1.0 + spread_weight * (compliance - center) / spread) / compliance.shape[0]

def reference(displacements, connectivity, density, stiffness, filter_inverse, send_rows, send_count, recv_cell):
    nodal = displacements.reshape(SAMPLES, 3, SLABS, NODES_DEV)
    linked = connectivity.reshape(8, SLABS, E_DEV)

    def slab_energy(slab_id):
        slab_nodal = lax.dynamic_index_in_dim(nodal, slab_id, 2, keepdims=False)
        slab_links = lax.dynamic_index_in_dim(linked, slab_id, 1, keepdims=False)

        def sample_energy(sample_nodal):
            gathered = sample_nodal[:, slab_links].reshape(24, E_DEV)
            applied = jnp.dot(stiffness, gathered, preferred_element_type=jnp.float32)
            return lax.optimization_barrier(jnp.sum(gathered.astype(jnp.float32) * applied, axis=0))
        return lax.map(sample_energy, slab_nodal)
    energy = lax.map(slab_energy, jnp.arange(SLABS, dtype=jnp.int32))
    solid_frac = density.reshape(SLABS, E_DEV)
    compliance = jnp.einsum('jse,je->s', energy, solid_frac ** 3, precision=lax.Precision.HIGHEST) / ELEMS
    weight = robust_weights(compliance)
    sensitivity = -penalty * solid_frac ** 2 * jnp.einsum('jse,s->je', energy, weight, precision=lax.Precision.HIGHEST)
    mean_energy = lax.optimization_barrier(jnp.sum(energy, axis=1)) / SAMPLES
    slab_ids = jnp.arange(SLABS, dtype=jnp.int32)[:, None, None, None]
    group_ids = jnp.arange(GROUPS, dtype=jnp.int32)[None, :, None, None]
    flat_ids = slab_ids * E_DEV + group_ids * EB + send_rows
    slot_ids = jnp.arange(CAP, dtype=jnp.int32)[None, None, None, :]
    live_mask = slot_ids < send_count[..., None]
    owner_ids = jnp.arange(GROUPS, dtype=jnp.int32)[:, None] * SLABS + jnp.arange(SLABS, dtype=jnp.int32)[None, :]
    target_ids = (owner_ids[:, :, None, None] * EB + recv_cell).reshape(-1)

    def assemble(field):
        picked = jnp.where(live_mask, field.reshape(-1)[flat_ids], jnp.zeros((), field.dtype))
        arrived = jnp.transpose(picked, (1, 2, 0, 3)).reshape(-1)
        return jnp.zeros((GROUPS * SLABS * EB,), field.dtype).at[target_ids].add(arrived)

    def smooth(node_field):
        patches = node_field.reshape(GROUPS * SLABS, EB // PATCH, PATCH)
        result = jnp.einsum('gpb,ab->gpa', patches, filter_inverse, precision=lax.Precision.HIGHEST)
        return result.reshape(GROUPS, SLABS, EB)
    return (compliance, smooth(assemble(sensitivity)), smooth(assemble(mean_energy)))
```

```python
import functools

import jax
import jax.numpy as jnp
from jax import lax
from jax.experimental import pallas as pl
from jax.experimental.pallas import tpu as pltpu
from jax.sharding import PartitionSpec as P

penalty = 3.0
spread_weight = 0.5
epsilon = 1e-06

LANES = 128
BLOCK = 1024
UNROLL = 32
CHUNK = 256
ROWS = 16
F32 = jnp.float32
BF16 = jnp.bfloat16


def energy_kernel(steps, place_ref, *refs):
    links = refs[:8]
    own_ref, other_ref, weight_ref, density_ref = refs[8:12]
    out_refs, parts_ref = refs[12:16], refs[16]
    table, rows, total = refs[17:]
    turn, sub = pl.program_id(0), pl.program_id(1)
    nodes = table.shape[0]

    @pl.when((turn == 0) & (sub == 0))
    def _():
        total[...] = jnp.zeros_like(total)
        pad = jnp.zeros((ROWS, LANES), F32)

        def fill(n, _):
            at = pl.ds(pl.multiple_of(n * LANES, LANES), LANES)
            own, other = own_ref[:, at], other_ref[:, at]
            half = []
            for k in range(3):
                half += [own[8 * k : 8 * k + 8], other[8 * k : 8 * k + 8]]
            half.append(pad)
            table[at, :] = jnp.concatenate(half + half, axis=0).T
            return 0

        lax.fori_loop(0, nodes // LANES, fill, 0)

    first_half = lax.broadcasted_iota(jnp.int32, (1, LANES), 1) < LANES // 2

    def gather(t, _):
        start = pl.multiple_of(t * UNROLL, UNROLL)
        view = rows.at[pl.ds(start, UNROLL)]
        for u in range(UNROLL):
            e = start + u
            for p in range(4):
                low = table[pl.ds(links[2 * p][e], 1), :]
                high = table[pl.ds(links[2 * p + 1][e], 1), :]
                view[u : u + 1, p * LANES : (p + 1) * LANES] = jnp.where(first_half, low, high)
        return 0

    lax.fori_loop(0, BLOCK // UNROLL, gather, 0)

    acc = total[...]
    for chunk in range(BLOCK // CHUNK):
        field = rows[chunk * CHUNK : (chunk + 1) * CHUNK, :]
        applied = jnp.dot(field.astype(BF16), weight_ref[...], preferred_element_type=F32)
        product = field * applied
        folded = product[:, :LANES]
        for p in range(1, 4):
            folded = folded + product[:, p * LANES : (p + 1) * LANES]
        turned = folded.T
        half = turned[: LANES // 2] + turned[LANES // 2 :]
        energy = half[:ROWS] + half[ROWS : 2 * ROWS] + half[2 * ROWS : 3 * ROWS]
        at = pl.ds(pl.multiple_of(sub * BLOCK + chunk * CHUNK, CHUNK), CHUNK)
        for d in range(4):

            @pl.when(turn == d)
            def _(d=d):
                out_refs[d][:, at] = energy

        rho = density_ref[0, :, chunk * CHUNK : (chunk + 1) * CHUNK]
        scaled = energy * (rho * rho * rho)
        for p in range(CHUNK // LANES):
            acc = acc + scaled[:, p * LANES : (p + 1) * LANES]
    total[...] = acc

    @pl.when((turn == 3) & (sub == steps - 1))
    def _():
        column = jnp.sum(acc, axis=1, keepdims=True)
        row_id = lax.broadcasted_iota(jnp.int32, (ROWS, 64), 0)
        lane = lax.broadcasted_iota(jnp.int32, (ROWS, 64), 1)
        spot = jnp.where(row_id < 8, place_ref[4] * 8 + row_id, place_ref[5] * 8 + row_id - 8)
        row = jnp.sum(jnp.where(lane == spot, column, 0.0), axis=0, keepdims=True)
        parts_ref[...] = jnp.broadcast_to(row, parts_ref.shape)


def split(x):
    high = x.astype(BF16)
    return high, (x - high.astype(F32)).astype(BF16)


def send_kernel(elements, place_ref, count_ref, parts_ref, e0, e1, e2, e3, density_ref, picks_ref, comp_ref, out_ref):
    comp = jnp.sum(parts_ref[...], axis=0, keepdims=True) / elements
    comp_ref[...] = comp
    center = jnp.mean(comp, axis=1, keepdims=True)
    spread = jnp.sqrt(jnp.mean((comp - center) ** 2, axis=1, keepdims=True) + epsilon)
    weight = (1.0 + spread_weight * (comp - center) / spread) / 64.0
    row_id = lax.broadcasted_iota(jnp.int32, (8, 64), 0)
    lane = lax.broadcasted_iota(jnp.int32, (8, 64), 1)
    sens = mean = None
    for d, e_ref in enumerate((e0, e1, e2, e3)):
        for h in range(2):
            spot = place_ref[6 + 2 * d + h] * 8 + row_id
            column = jnp.sum(jnp.where(lane == spot, weight, 0.0), axis=1, keepdims=True)
            field = e_ref[8 * h : 8 * h + 8, :]
            term = column * field
            sens = term if sens is None else sens + term
            mean = field if mean is None else mean + field
    rho = density_ref[0]
    sens = -penalty * rho * rho * jnp.sum(sens, axis=0, keepdims=True)
    mean = jnp.sum(mean, axis=0, keepdims=True) / 64.0
    both = [f[:, h * LANES : (h + 1) * LANES] for f in (sens, mean) for h in range(16)]
    table = jnp.concatenate(split(jnp.concatenate(both, axis=0)), axis=0)
    width = picks_ref.shape[2]
    low_id = lax.broadcasted_iota(jnp.int32, (LANES, width), 0)
    high_id = lax.broadcasted_iota(jnp.int32, (16, width), 0)
    slot = lax.broadcasted_iota(jnp.int32, (16, width), 1)
    for d in range(picks_ref.shape[1]):
        pick = picks_ref[0, d : d + 1, :]
        hot = jnp.where(low_id == (pick & (LANES - 1)), 1.0, 0.0).astype(BF16)
        found = jnp.dot(table, hot, preferred_element_type=F32)
        found = found[:32] + found[32:]
        live = (high_id == (pick >> 7)) & (slot < count_ref[place_ref[0] * 16 + d])
        for f in range(2):
            got = jnp.sum(jnp.where(live, found[16 * f : 16 * f + 16], 0.0), axis=0, keepdims=True)
            for p in range(width // LANES):
                r = f * (width // LANES) + p
                out_ref[d, r : r + 1, :] = got[:, p * LANES : (p + 1) * LANES]


def owner_kernel(got_ref, cells_ref, filter_ref, sens_ref, energy_ref):
    sources, width = cells_ref.shape[2], cells_ref.shape[3]
    low_id = lax.broadcasted_iota(jnp.int32, (LANES, width), 0)
    high_id = lax.broadcasted_iota(jnp.int32, (16, width), 0)
    node = jnp.zeros((64, LANES), F32)
    for j in range(sources):
        cell = cells_ref[0, 0, j : j + 1, :]
        hot = jnp.where(low_id == (cell & (LANES - 1)), 1.0, 0.0).astype(BF16)
        mine = high_id == (cell >> 7)
        pieces = []
        for f in range(2):
            value = jnp.concatenate([got_ref[j, 2 * f : 2 * f + 1, :], got_ref[j, 2 * f + 1 : 2 * f + 2, :]], axis=1)
            pieces.append(jnp.where(mine, value, 0.0))
        rows = jnp.concatenate(split(jnp.concatenate(pieces, axis=0)), axis=0)
        node = node + lax.dot_general(rows, hot, (((1,), (1,)), ((), ())), preferred_element_type=F32)
    node = node[:32] + node[32:]
    result = lax.dot_general(
        node, filter_ref[...], (((1,), (1,)), ((), ())),
        precision=lax.Precision.HIGHEST, preferred_element_type=F32,
    )
    for p in range(16):
        sens_ref[0, :, p * LANES : (p + 1) * LANES] = result[p : p + 1]
        energy_ref[0, :, p * LANES : (p + 1) * LANES] = result[16 + p : 17 + p]


def block_stiffness(stiffness):
    lane = jnp.arange(512, dtype=jnp.int32)
    spot = lane % 64
    corner = 2 * (lane // LANES) + (lane % LANES) // 64
    dof = jnp.where(spot < 48, 8 * (spot // ROWS) + corner, -1)
    hot = (dof[:, None] == jnp.arange(24, dtype=jnp.int32)[None, :]).astype(BF16)
    wide = jnp.dot(hot, jnp.dot(stiffness.T, hot.T, preferred_element_type=F32).astype(BF16), preferred_element_type=F32)
    same = (lane % ROWS)[:, None] == (lane % ROWS)[None, :]
    return jnp.where(same, wide, 0.0).astype(BF16)


def body(displacements, connectivity, density, stiffness, filter_inverse, send_rows, send_count, recv_cell):
    group_id = lax.axis_index("sample")
    z, core = group_id // 2, group_id % 2
    node_count = displacements.shape[2]
    elements = density.shape[0]
    groups = 8
    sub_rows = elements // groups
    slabs = lax.axis_size("space")
    nodes = (node_count + LANES - 1) // LANES * LANES

    own = jnp.transpose(displacements, (1, 0, 2)).reshape(24, node_count).astype(F32)
    own = jnp.pad(own, ((0, 0), (0, nodes - node_count)))
    other = lax.ppermute(own, "sample", [(i, i ^ 1) for i in range(8)])
    links = connectivity.reshape(-1)
    rho = density.reshape(groups, 1, sub_rows)
    weights = block_stiffness(stiffness)

    order = (1, 2, 3, 0)
    place = [2 * ((z + d) % 4) + core for d in order] + [group_id, group_id ^ 1]
    steps = sub_rows // BLOCK
    per_corner = elements // BLOCK

    def link_spec(c):
        return pl.BlockSpec(
            (BLOCK,), lambda t, s, at: (c * per_corner + at[t] * steps + s,), memory_space=pltpu.SMEM
        )

    whole = pl.BlockSpec(memory_space=pltpu.VMEM)
    energies = pl.pallas_call(
        functools.partial(energy_kernel, steps),
        grid_spec=pltpu.PrefetchScalarGridSpec(
            num_scalar_prefetch=1,
            grid=(4, steps),
            in_specs=[link_spec(c) for c in range(8)]
            + [whole, whole, whole, pl.BlockSpec((1, 1, BLOCK), lambda t, s, at: (at[t], 0, s))],
            out_specs=[whole] * 5,
            scratch_shapes=[
                pltpu.VMEM((nodes, LANES), F32),
                pltpu.VMEM((BLOCK, 4 * LANES), F32),
                pltpu.VMEM((ROWS, LANES), F32),
            ],
        ),
        out_shape=[jax.ShapeDtypeStruct((ROWS, sub_rows), F32)] * 4 + [jax.ShapeDtypeStruct((128, 64), F32)],
        compiler_params=pltpu.CompilerParams(vmem_limit_bytes=48 * 2**20),
        name="energy",
    )(jnp.stack(place).astype(jnp.int32), *([links] * 8), own, other, weights, rho)
    parts = lax.all_to_all(energies[4], ("sample", "space"), split_axis=0, concat_axis=0, tiled=True)
    arrived = [energies[3]] + [
        lax.ppermute(energies[d - 1], "sample", [(i, (i + 2 * d) % 8) for i in range(8)]) for d in (1, 2, 3)
    ]
    source = [2 * ((z - d) % 4) for d in range(4)]
    place2 = [group_id] * 6
    for base in source:
        place2 += [base + core, base + 1 - core]

    smem = pl.BlockSpec(memory_space=pltpu.SMEM)
    width = send_rows.shape[-1]
    compliance, outgoing = pl.pallas_call(
        functools.partial(send_kernel, float(elements * slabs)),
        in_specs=[smem, smem] + [whole] * 7,
        out_specs=[whole] * 2,
        out_shape=[
            jax.ShapeDtypeStruct((1, 64), F32),
            jax.ShapeDtypeStruct((slabs, 2 * width // LANES, LANES), F32),
        ],
        name="send",
    )(
        jnp.stack(place2).astype(jnp.int32),
        send_count.reshape(-1),
        parts,
        *arrived,
        lax.dynamic_slice_in_dim(rho, group_id, 1, 0),
        lax.dynamic_slice_in_dim(send_rows[0], group_id, 1, 0),
    )
    got = lax.all_to_all(outgoing, "space", split_axis=0, concat_axis=0, tiled=True)
    sens, energy = pl.pallas_call(
        owner_kernel,
        in_specs=[whole] * 3,
        out_specs=[whole] * 2,
        out_shape=[jax.ShapeDtypeStruct((1, 1, sub_rows), F32)] * 2,
        name="owner",
    )(got, recv_cell, filter_inverse)
    return (compliance.reshape(-1), sens, energy)


def solution(mesh):
    in_specs = (
        P("sample", None, "space"),
        P(None, "space"),
        P("space"),
        P(),
        P(),
        P("space", None, None, None),
        P("space", None, None),
        P("sample", "space", None, None),
    )
    out_specs = (P(), P("sample", "space", None), P("sample", "space", None))
    return jax.shard_map(body, mesh=mesh, in_specs=in_specs, out_specs=out_specs, check_vma=False)
```

```python
import functools

import jax
import jax.numpy as jnp
from jax import lax
from jax.experimental import pallas as pl
from jax.experimental.pallas import tpu as pltpu
from jax.sharding import PartitionSpec as P

penalty = 3.0
spread_weight = 0.5
epsilon = 1e-06

LANES = 128
BLOCK = 1024
FILL = 29
UNROLL = 32
ROWS = 16
F32 = jnp.float32
BF16 = jnp.bfloat16


def energy_kernel(steps, place_ref, *refs):
    links = refs[:8]
    own_ref, other_ref, weight_ref, density_ref = refs[8:12]
    out_refs, parts_ref = refs[12:16], refs[16]
    table, rows, total = refs[17:]
    turn, sub = pl.program_id(0), pl.program_id(1)
    nodes = table.shape[0]

    @pl.when((turn == 0) & (sub == 0))
    def _():
        total[...] = jnp.zeros_like(total)
        pad = jnp.zeros((ROWS, LANES), F32)

        def fill(n, _):
            start = pl.multiple_of(n * (FILL * LANES), LANES)
            for i in range(FILL):
                at = pl.ds(start + i * LANES, LANES)
                own, other = own_ref[:, at], other_ref[:, at]
                half = []
                for k in range(3):
                    half += [own[8 * k : 8 * k + 8], other[8 * k : 8 * k + 8]]
                half.append(pad)
                table[at, :] = jnp.concatenate(half + half, axis=0).T
            return 0

        lax.fori_loop(0, nodes // (FILL * LANES), fill, 0)

    first_half = lax.broadcasted_iota(jnp.int32, (1, LANES), 1) < LANES // 2

    def gather(t, _):
        start = pl.multiple_of(t * UNROLL, UNROLL)
        view = rows.at[pl.ds(start, UNROLL)]
        for u in range(UNROLL):
            e = start + u
            for p in range(4):
                low = table[pl.ds(links[2 * p][e], 1), :]
                high = table[pl.ds(links[2 * p + 1][e], 1), :]
                view[u : u + 1, p * LANES : (p + 1) * LANES] = jnp.where(first_half, low, high)
        return 0

    lax.fori_loop(0, BLOCK // UNROLL, gather, 0)

    field = rows[...]
    applied = jnp.dot(field.astype(BF16), weight_ref[...], preferred_element_type=F32)
    product = field * applied
    folded = product[:, :LANES]
    for p in range(1, 4):
        folded = folded + product[:, p * LANES : (p + 1) * LANES]
    turned = folded.T
    half = turned[: LANES // 2] + turned[LANES // 2 :]
    energy = half[:ROWS] + half[ROWS : 2 * ROWS] + half[2 * ROWS : 3 * ROWS]
    at = pl.ds(pl.multiple_of(sub * BLOCK, BLOCK), BLOCK)
    for d in range(4):

        @pl.when(turn == d)
        def _(d=d):
            out_refs[d][:, at] = energy

    rho = density_ref[0]
    scaled = energy * (rho * rho * rho)
    acc = total[...]
    for p in range(BLOCK // LANES):
        acc = acc + scaled[:, p * LANES : (p + 1) * LANES]
    total[...] = acc

    @pl.when((turn == 3) & (sub == steps - 1))
    def _():
        column = jnp.sum(acc, axis=1, keepdims=True)
        row_id = lax.broadcasted_iota(jnp.int32, (ROWS, 64), 0)
        lane = lax.broadcasted_iota(jnp.int32, (ROWS, 64), 1)
        spot = jnp.where(row_id < 8, place_ref[4] * 8 + row_id, place_ref[5] * 8 + row_id - 8)
        row = jnp.sum(jnp.where(lane == spot, column, 0.0), axis=0, keepdims=True)
        parts_ref[...] = jnp.broadcast_to(row, parts_ref.shape)


def split(x):
    high = x.astype(BF16)
    return high, (x - high.astype(F32)).astype(BF16)


def prepare_kernel(place_ref, count_ref, picks_ref, *refs):
    hot_ref, live_ref = refs[-2:]
    dests, width = picks_ref.shape[1:]
    low_id = lax.broadcasted_iota(jnp.int32, (LANES, width), 0)
    high_id = lax.broadcasted_iota(jnp.int32, (16, width), 0)
    slot = lax.broadcasted_iota(jnp.int32, (16, width), 1)
    for d in range(dests):
        pick = picks_ref[0, d : d + 1, :]
        hot_ref[d] = jnp.where(low_id == (pick & (LANES - 1)), 1.0, 0.0).astype(BF16)
        live = (high_id == (pick >> 7)) & (slot < count_ref[place_ref[0] * 16 + d])
        live_ref[d] = jnp.where(live, 1.0, 0.0)


def send_kernel(elements, place_ref, parts_ref, e0, e1, e2, e3, density_ref, hot_ref, live_ref, comp_ref, out_ref):
    comp = jnp.sum(parts_ref[...], axis=0, keepdims=True) / elements
    comp_ref[...] = comp
    center = jnp.mean(comp, axis=1, keepdims=True)
    spread = jnp.sqrt(jnp.mean((comp - center) ** 2, axis=1, keepdims=True) + epsilon)
    weight = (1.0 + spread_weight * (comp - center) / spread) / 64.0
    row_id = lax.broadcasted_iota(jnp.int32, (8, 64), 0)
    lane = lax.broadcasted_iota(jnp.int32, (8, 64), 1)
    sens = mean = None
    for d, e_ref in enumerate((e0, e1, e2, e3)):
        for h in range(2):
            spot = place_ref[6 + 2 * d + h] * 8 + row_id
            column = jnp.sum(jnp.where(lane == spot, weight, 0.0), axis=1, keepdims=True)
            field = e_ref[8 * h : 8 * h + 8, :]
            term = column * field
            sens = term if sens is None else sens + term
            mean = field if mean is None else mean + field
    rho = density_ref[0]
    sens = -penalty * rho * rho * jnp.sum(sens, axis=0, keepdims=True)
    mean = jnp.sum(mean, axis=0, keepdims=True) / 64.0
    both = [f[:, h * LANES : (h + 1) * LANES] for f in (sens, mean) for h in range(16)]
    table = jnp.concatenate(split(jnp.concatenate(both, axis=0)), axis=0)
    dests, _, width = hot_ref.shape
    for d in range(dests):
        found = jnp.dot(table, hot_ref[d], preferred_element_type=F32)
        found = found[:32] + found[32:]
        for f in range(2):
            got = jnp.sum(found[16 * f : 16 * f + 16] * live_ref[d], axis=0, keepdims=True)
            for p in range(width // LANES):
                r = f * (width // LANES) + p
                out_ref[d, r : r + 1, :] = got[:, p * LANES : (p + 1) * LANES]


def owner_kernel(got_ref, cells_ref, filter_ref, sens_ref, energy_ref):
    sources, width = cells_ref.shape[2], cells_ref.shape[3]
    low_id = lax.broadcasted_iota(jnp.int32, (LANES, width), 0)
    high_id = lax.broadcasted_iota(jnp.int32, (16, width), 0)
    node = jnp.zeros((64, LANES), F32)
    for j in range(sources):
        cell = cells_ref[0, 0, j : j + 1, :]
        hot = jnp.where(low_id == (cell & (LANES - 1)), 1.0, 0.0).astype(BF16)
        mine = high_id == (cell >> 7)
        pieces = []
        for f in range(2):
            value = jnp.concatenate([got_ref[j, 2 * f : 2 * f + 1, :], got_ref[j, 2 * f + 1 : 2 * f + 2, :]], axis=1)
            pieces.append(jnp.where(mine, value, 0.0))
        rows = jnp.concatenate(split(jnp.concatenate(pieces, axis=0)), axis=0)
        node = node + lax.dot_general(rows, hot, (((1,), (1,)), ((), ())), preferred_element_type=F32)
    node = node[:32] + node[32:]
    result = lax.dot_general(
        node, filter_ref[...], (((1,), (1,)), ((), ())),
        precision=lax.Precision.HIGHEST, preferred_element_type=F32,
    )
    for p in range(16):
        sens_ref[0, :, p * LANES : (p + 1) * LANES] = result[p : p + 1]
        energy_ref[0, :, p * LANES : (p + 1) * LANES] = result[16 + p : 17 + p]


def block_stiffness(stiffness):
    lane = jnp.arange(512, dtype=jnp.int32)
    spot = lane % 64
    corner = 2 * (lane // LANES) + (lane % LANES) // 64
    dof = jnp.where(spot < 48, 8 * (spot // ROWS) + corner, -1)
    hot = (dof[:, None] == jnp.arange(24, dtype=jnp.int32)[None, :]).astype(BF16)
    wide = jnp.dot(hot, jnp.dot(stiffness.T, hot.T, preferred_element_type=F32).astype(BF16), preferred_element_type=F32)
    same = (lane % ROWS)[:, None] == (lane % ROWS)[None, :]
    return jnp.where(same, wide, 0.0).astype(BF16)


def body(displacements, connectivity, density, stiffness, filter_inverse, send_rows, send_count, recv_cell):
    group_id = lax.axis_index("sample")
    z, core = group_id // 2, group_id % 2
    node_count = displacements.shape[2]
    elements = density.shape[0]
    groups = 8
    sub_rows = elements // groups
    slabs = lax.axis_size("space")
    nodes = (node_count + LANES - 1) // LANES * LANES

    own = jnp.transpose(displacements, (1, 0, 2)).reshape(24, node_count).astype(F32)
    own = jnp.pad(own, ((0, 0), (0, nodes - node_count)))
    other = lax.ppermute(own, "sample", [(i, i ^ 1) for i in range(8)])
    links = connectivity.reshape(-1)
    rho = density.reshape(groups, 1, sub_rows)
    weights = block_stiffness(stiffness)

    order = (1, 2, 3, 0)
    place = [2 * ((z + d) % 4) + core for d in order] + [group_id, group_id ^ 1]
    steps = sub_rows // BLOCK
    per_corner = elements // BLOCK

    def link_spec(c):
        return pl.BlockSpec(
            (BLOCK,), lambda t, s, at: (c * per_corner + at[t] * steps + s,), memory_space=pltpu.SMEM
        )

    whole = pl.BlockSpec(memory_space=pltpu.VMEM)
    energies = pl.pallas_call(
        functools.partial(energy_kernel, steps),
        grid_spec=pltpu.PrefetchScalarGridSpec(
            num_scalar_prefetch=1,
            grid=(4, steps),
            in_specs=[link_spec(c) for c in range(8)]
            + [whole, whole, whole, pl.BlockSpec((1, 1, BLOCK), lambda t, s, at: (at[t], 0, s))],
            out_specs=[whole] * 5,
            scratch_shapes=[
                pltpu.VMEM((nodes, LANES), F32),
                pltpu.VMEM((BLOCK, 4 * LANES), F32),
                pltpu.VMEM((ROWS, LANES), F32),
            ],
        ),
        out_shape=[jax.ShapeDtypeStruct((ROWS, sub_rows), F32)] * 4 + [jax.ShapeDtypeStruct((128, 64), F32)],
        compiler_params=pltpu.CompilerParams(vmem_limit_bytes=48 * 2**20),
        name="energy",
    )(jnp.stack(place).astype(jnp.int32), *([links] * 8), own, other, weights, rho)
    parts = lax.all_to_all(energies[4], ("sample", "space"), split_axis=0, concat_axis=0, tiled=True)
    source = [2 * ((z - d) % 4) for d in range(4)]
    place2 = [group_id] * 6
    for base in source:
        place2 += [base + core, base + 1 - core]
    place2 = jnp.stack(place2).astype(jnp.int32)

    smem = pl.BlockSpec(memory_space=pltpu.SMEM)
    stay = pl.BlockSpec(memory_space=pl.ANY)
    width = send_rows.shape[-1]
    e1, e2, e3, hot, live = pl.pallas_call(
        prepare_kernel,
        in_specs=[smem, smem, whole, stay, stay, stay],
        out_specs=[stay, stay, stay, whole, whole],
        out_shape=[jax.ShapeDtypeStruct((ROWS, sub_rows), F32)] * 3
        + [jax.ShapeDtypeStruct((slabs, LANES, width), BF16), jax.ShapeDtypeStruct((slabs, 16, width), F32)],
        input_output_aliases={3: 0, 4: 1, 5: 2},
        cost_estimate=pl.CostEstimate(flops=4 * 10**9, bytes_accessed=2**21, transcendentals=0),
        name="prepare",
    )(
        place2,
        send_count.reshape(-1),
        lax.dynamic_slice_in_dim(send_rows[0], group_id, 1, 0),
        *energies[:3],
    )
    arrived = [energies[3]] + [
        lax.ppermute(e, "sample", [(i, (i + 2 * d) % 8) for i in range(8)]) for d, e in ((1, e1), (2, e2), (3, e3))
    ]
    compliance, outgoing = pl.pallas_call(
        functools.partial(send_kernel, float(elements * slabs)),
        in_specs=[smem] + [whole] * 8,
        out_specs=[whole] * 2,
        out_shape=[
            jax.ShapeDtypeStruct((1, 64), F32),
            jax.ShapeDtypeStruct((slabs, 2 * width // LANES, LANES), F32),
        ],
        name="send",
    )(place2, parts, *arrived, lax.dynamic_slice_in_dim(rho, group_id, 1, 0), hot, live)
    got = lax.all_to_all(outgoing, "space", split_axis=0, concat_axis=0, tiled=True)
    sens, energy = pl.pallas_call(
        owner_kernel,
        in_specs=[whole] * 3,
        out_specs=[whole] * 2,
        out_shape=[jax.ShapeDtypeStruct((1, 1, sub_rows), F32)] * 2,
        name="owner",
    )(got, recv_cell, filter_inverse)
    return (compliance.reshape(-1), sens, energy)


def solution(mesh):
    in_specs = (
        P("sample", None, "space"),
        P(None, "space"),
        P("space"),
        P(),
        P(),
        P("space", None, None, None),
        P("space", None, None),
        P("sample", "space", None, None),
    )
    out_specs = (P(), P("sample", "space", None), P("sample", "space", None))
    return jax.shard_map(body, mesh=mesh, in_specs=in_specs, out_specs=out_specs, check_vma=False)
```

```python
import functools

import jax
import jax.numpy as jnp
from jax import lax
from jax.experimental import pallas as pl
from jax.experimental.pallas import tpu as pltpu
from jax.sharding import PartitionSpec as P

penalty = 3.0
spread_weight = 0.5
epsilon = 1e-06

LANES = 128
BLOCK = 1024
FILL = 29
UNROLL = 32
ROWS = 16
F32 = jnp.float32
BF16 = jnp.bfloat16


def energy_kernel(steps, place_ref, *refs):
    links = refs[:8]
    own_ref, other_ref, weight_ref, density_ref = refs[8:12]
    out_ref, parts_ref = refs[12:14]
    table, rows, total = refs[14:]
    turn, sub = pl.program_id(0), pl.program_id(1)
    nodes = table.shape[0]

    @pl.when((turn == 0) & (sub == 0))
    def _():
        total[...] = jnp.zeros_like(total)
        pad = jnp.zeros((ROWS, LANES), F32)

        def fill(n, _):
            start = pl.multiple_of(n * (FILL * LANES), LANES)
            for i in range(FILL):
                at = pl.ds(start + i * LANES, LANES)
                own, other = own_ref[:, at], other_ref[:, at]
                half = []
                for k in range(3):
                    half += [own[8 * k : 8 * k + 8], other[8 * k : 8 * k + 8]]
                half.append(pad)
                table[at, :] = jnp.concatenate(half + half, axis=0).T
            return 0

        lax.fori_loop(0, nodes // (FILL * LANES), fill, 0)

    first_half = lax.broadcasted_iota(jnp.int32, (1, LANES), 1) < LANES // 2

    def gather(t, _):
        start = pl.multiple_of(t * UNROLL, UNROLL)
        view = rows.at[pl.ds(start, UNROLL)]
        for u in range(UNROLL):
            e = start + u
            for p in range(4):
                low = table[pl.ds(links[2 * p][e], 1), :]
                high = table[pl.ds(links[2 * p + 1][e], 1), :]
                view[u : u + 1, p * LANES : (p + 1) * LANES] = jnp.where(first_half, low, high)
        return 0

    lax.fori_loop(0, BLOCK // UNROLL, gather, 0)

    field = rows[...]
    applied = jnp.dot(field.astype(BF16), weight_ref[...], preferred_element_type=F32)
    product = field * applied
    folded = product[:, :LANES]
    for p in range(1, 4):
        folded = folded + product[:, p * LANES : (p + 1) * LANES]
    turned = folded.T
    half = turned[: LANES // 2] + turned[LANES // 2 :]
    energy = half[:ROWS] + half[ROWS : 2 * ROWS] + half[2 * ROWS : 3 * ROWS]
    out_ref[0] = energy
    rho = density_ref[0]
    scaled = energy * (rho * rho * rho)
    acc = total[...]
    for p in range(BLOCK // LANES):
        acc = acc + scaled[:, p * LANES : (p + 1) * LANES]
    total[...] = acc

    @pl.when((turn == 3) & (sub == steps - 1))
    def _():
        column = jnp.sum(acc, axis=1, keepdims=True)
        row_id = lax.broadcasted_iota(jnp.int32, (ROWS, 64), 0)
        lane = lax.broadcasted_iota(jnp.int32, (ROWS, 64), 1)
        spot = jnp.where(row_id < 8, place_ref[4] * 8 + row_id, place_ref[5] * 8 + row_id - 8)
        row = jnp.sum(jnp.where(lane == spot, column, 0.0), axis=0, keepdims=True)
        parts_ref[...] = jnp.broadcast_to(row, parts_ref.shape)


def split(x):
    high = x.astype(BF16)
    return high, (x - high.astype(F32)).astype(BF16)


def send_kernel(elements, place_ref, count_ref, parts_ref, energy_ref, density_ref, picks_ref, comp_ref, out_ref):
    comp = jnp.sum(parts_ref[...], axis=0, keepdims=True) / elements
    comp_ref[...] = comp
    center = jnp.mean(comp, axis=1, keepdims=True)
    spread = jnp.sqrt(jnp.mean((comp - center) ** 2, axis=1, keepdims=True) + epsilon)
    weight = (1.0 + spread_weight * (comp - center) / spread) / 64.0
    row_id = lax.broadcasted_iota(jnp.int32, (ROWS, 64), 0)
    lane = lax.broadcasted_iota(jnp.int32, (ROWS, 64), 1)
    spot = jnp.where(row_id < 8, place_ref[4] * 8 + row_id, place_ref[5] * 8 + row_id - 8)
    column = jnp.sum(jnp.where(lane == spot, weight, 0.0), axis=1, keepdims=True)
    _, dests, width = picks_ref.shape
    low_id = lax.broadcasted_iota(jnp.int32, (LANES, width), 0)
    high_id = lax.broadcasted_iota(jnp.int32, (16, width), 0)
    slot = lax.broadcasted_iota(jnp.int32, (16, width), 1)
    for q in range(4):
        energy = energy_ref[q]
        rho = density_ref[place_ref[q]]
        sens = -penalty * rho * rho * jnp.sum(column * energy, axis=0, keepdims=True)
        mean = jnp.sum(energy, axis=0, keepdims=True) / 64.0
        both = [f[:, h * LANES : (h + 1) * LANES] for f in (sens, mean) for h in range(16)]
        table = jnp.concatenate(split(jnp.concatenate(both, axis=0)), axis=0)
        for d in range(dests):
            pick = picks_ref[q, d : d + 1, :]
            hot = jnp.where(low_id == (pick & (LANES - 1)), 1.0, 0.0).astype(BF16)
            found = jnp.dot(table, hot, preferred_element_type=F32)
            found = found[:32] + found[32:]
            live = (high_id == (pick >> 7)) & (slot < count_ref[place_ref[q] * 16 + d])
            for f in range(2):
                got = jnp.sum(jnp.where(live, found[16 * f : 16 * f + 16], 0.0), axis=0, keepdims=True)
                for p in range(width // LANES):
                    r = f * (width // LANES) + p
                    out_ref[q * dests + d, r : r + 1, :] = got[:, p * LANES : (p + 1) * LANES]


def owner_kernel(got_ref, cells_ref, filter_ref, sens_ref, energy_ref):
    sources, width = cells_ref.shape[2], cells_ref.shape[3]
    low_id = lax.broadcasted_iota(jnp.int32, (LANES, width), 0)
    high_id = lax.broadcasted_iota(jnp.int32, (16, width), 0)
    node = jnp.zeros((64, LANES), F32)
    for j in range(sources):
        cell = cells_ref[0, 0, j : j + 1, :]
        hot = jnp.where(low_id == (cell & (LANES - 1)), 1.0, 0.0).astype(BF16)
        mine = high_id == (cell >> 7)
        pieces = []
        share = got_ref[j]
        for q in range(1, 4):
            share = share + got_ref[q * sources + j]
        for f in range(2):
            value = jnp.concatenate([share[2 * f : 2 * f + 1], share[2 * f + 1 : 2 * f + 2]], axis=1)
            pieces.append(jnp.where(mine, value, 0.0))
        rows = jnp.concatenate(split(jnp.concatenate(pieces, axis=0)), axis=0)
        node = node + lax.dot_general(rows, hot, (((1,), (1,)), ((), ())), preferred_element_type=F32)
    node = node[:32] + node[32:]
    result = lax.dot_general(
        node, filter_ref[...], (((1,), (1,)), ((), ())),
        precision=lax.Precision.HIGHEST, preferred_element_type=F32,
    )
    for p in range(16):
        sens_ref[0, :, p * LANES : (p + 1) * LANES] = result[p : p + 1]
        energy_ref[0, :, p * LANES : (p + 1) * LANES] = result[16 + p : 17 + p]


def block_stiffness(stiffness):
    lane = jnp.arange(512, dtype=jnp.int32)
    spot = lane % 64
    corner = 2 * (lane // LANES) + (lane % LANES) // 64
    dof = jnp.where(spot < 48, 8 * (spot // ROWS) + corner, -1)
    hot = (dof[:, None] == jnp.arange(24, dtype=jnp.int32)[None, :]).astype(BF16)
    wide = jnp.dot(hot, jnp.dot(stiffness.T, hot.T, preferred_element_type=F32).astype(BF16), preferred_element_type=F32)
    same = (lane % ROWS)[:, None] == (lane % ROWS)[None, :]
    return jnp.where(same, wide, 0.0).astype(BF16)


def body(displacements, connectivity, density, stiffness, filter_inverse, send_rows, send_count, recv_cell):
    group_id = lax.axis_index("sample")
    core = group_id % 2
    node_count = displacements.shape[2]
    elements = density.shape[0]
    groups = 8
    sub_rows = elements // groups
    slabs = lax.axis_size("space")
    nodes = (node_count + LANES - 1) // LANES * LANES

    own = jnp.transpose(displacements, (1, 0, 2)).reshape(24, node_count).astype(F32)
    own = jnp.pad(own, ((0, 0), (0, nodes - node_count)))
    other = lax.ppermute(own, "sample", [(i, i ^ 1) for i in range(8)])
    links = connectivity.reshape(-1)
    rho = density.reshape(groups, 1, sub_rows)
    weights = block_stiffness(stiffness)

    place = jnp.stack([2 * q + core for q in range(4)] + [group_id, group_id ^ 1]).astype(jnp.int32)
    steps = sub_rows // BLOCK
    per_corner = elements // BLOCK

    def link_spec(c):
        return pl.BlockSpec(
            (BLOCK,), lambda t, s, at: (c * per_corner + at[t] * steps + s,), memory_space=pltpu.SMEM
        )

    whole = pl.BlockSpec(memory_space=pltpu.VMEM)
    energies, mine = pl.pallas_call(
        functools.partial(energy_kernel, steps),
        grid_spec=pltpu.PrefetchScalarGridSpec(
            num_scalar_prefetch=1,
            grid=(4, steps),
            in_specs=[link_spec(c) for c in range(8)]
            + [whole, whole, whole, pl.BlockSpec((1, 1, BLOCK), lambda t, s, at: (at[t], 0, s))],
            out_specs=[pl.BlockSpec((1, ROWS, BLOCK), lambda t, s, at: (t, 0, s)), whole],
            scratch_shapes=[
                pltpu.VMEM((nodes, LANES), F32),
                pltpu.VMEM((BLOCK, 4 * LANES), F32),
                pltpu.VMEM((ROWS, LANES), F32),
            ],
        ),
        out_shape=[jax.ShapeDtypeStruct((4, ROWS, sub_rows), F32), jax.ShapeDtypeStruct((128, 64), F32)],
        compiler_params=pltpu.CompilerParams(vmem_limit_bytes=48 * 2**20),
        name="energy",
    )(place, *([links] * 8), own, other, weights, rho)
    parts = lax.all_to_all(mine, ("sample", "space"), split_axis=0, concat_axis=0, tiled=True)
    smem = pl.BlockSpec(memory_space=pltpu.SMEM)
    dests, width = send_rows.shape[-2:]
    picks = lax.dynamic_index_in_dim(send_rows.reshape(4, 2, dests, width), core, 1, keepdims=False)
    compliance, outgoing = pl.pallas_call(
        functools.partial(send_kernel, float(elements * slabs)),
        in_specs=[smem, smem] + [whole] * 4,
        out_specs=[whole] * 2,
        out_shape=[
            jax.ShapeDtypeStruct((1, 64), F32),
            jax.ShapeDtypeStruct((4 * dests, 2 * width // LANES, LANES), F32),
        ],
        name="send",
    )(place, send_count.reshape(-1), parts, energies, rho, picks)
    peers = [[i * slabs + j for i in range(c, groups, 2) for j in range(slabs)] for c in range(2)]
    got = lax.all_to_all(
        outgoing, ("sample", "space"), split_axis=0, concat_axis=0, tiled=True, axis_index_groups=peers
    )
    sens, energy = pl.pallas_call(
        owner_kernel,
        in_specs=[whole] * 3,
        out_specs=[whole] * 2,
        out_shape=[jax.ShapeDtypeStruct((1, 1, sub_rows), F32)] * 2,
        name="owner",
    )(got, recv_cell, filter_inverse)
    return (compliance.reshape(-1), sens, energy)


def solution(mesh):
    in_specs = (
        P("sample", None, "space"),
        P(None, "space"),
        P("space"),
        P(),
        P(),
        P("space", None, None, None),
        P("space", None, None),
        P("sample", "space", None, None),
    )
    out_specs = (P(), P("sample", "space", None), P("sample", "space", None))
    return jax.shard_map(body, mesh=mesh, in_specs=in_specs, out_specs=out_specs, check_vma=False)
```

```python
import functools

import jax
import jax.numpy as jnp
from jax import lax
from jax.experimental import pallas as pl
from jax.experimental.pallas import tpu as pltpu
from jax.sharding import PartitionSpec as P

penalty = 3.0
spread_weight = 0.5
epsilon = 1e-06

LANES = 128
BLOCK = 2048
FILL = 29
UNROLL = 64
ROWS = 16
F32 = jnp.float32
BF16 = jnp.bfloat16


def energy_kernel(place_ref, links_ref, own_ref, other_ref, weight_ref, density_ref, out_ref, parts_ref, table, rows, *rest):
    links, sem = rest[:8], rest[8]
    elements = links_ref.shape[0] // 8
    copies = []
    for c in range(8):
        for q in range(4):
            start = pl.multiple_of(c * elements + place_ref[q] * BLOCK, BLOCK)
            copies.append(
                pltpu.make_async_copy(
                    links_ref.at[pl.ds(start, BLOCK)], links[c].at[pl.ds(q * BLOCK, BLOCK)], sem.at[c, q]
                )
            )
            copies[-1].start()

    pad = jnp.zeros((ROWS, LANES), F32)

    def fill(n, _):
        start = pl.multiple_of(n * (FILL * LANES), LANES)
        for i in range(FILL):
            at = pl.ds(start + i * LANES, LANES)
            own, other = own_ref[:, at], other_ref[:, at]
            half = []
            for k in range(3):
                half += [own[8 * k : 8 * k + 8], other[8 * k : 8 * k + 8]]
            half.append(pad)
            table[at, :] = jnp.concatenate(half + half, axis=0).T
        return 0

    lax.fori_loop(0, table.shape[0] // (FILL * LANES), fill, 0)
    for copy in copies:
        copy.wait()

    first_half = lax.broadcasted_iota(jnp.int32, (1, LANES), 1) < LANES // 2
    reach = 4 * BLOCK - UNROLL

    def group(q, acc):
        def gather(t, _):
            start = pl.multiple_of(t * UNROLL, UNROLL)
            view = rows.at[pl.ds(start, UNROLL)]
            e = q * BLOCK + start
            for u in range(UNROLL):
                for p in range(4):
                    low = table[pl.ds(links[2 * p].at[pl.ds(u, reach)][e], 1), :]
                    high = table[pl.ds(links[2 * p + 1].at[pl.ds(u, reach)][e], 1), :]
                    view[u : u + 1, p * LANES : (p + 1) * LANES] = jnp.where(first_half, low, high)
            return 0

        lax.fori_loop(0, BLOCK // UNROLL, gather, 0)
        field = rows[...]
        applied = jnp.dot(field.astype(BF16), weight_ref[...], preferred_element_type=F32)
        product = field * applied
        folded = product[:, :LANES]
        for p in range(1, 4):
            folded = folded + product[:, p * LANES : (p + 1) * LANES]
        turned = folded.T
        half = turned[: LANES // 2] + turned[LANES // 2 :]
        energy = half[:ROWS] + half[ROWS : 2 * ROWS] + half[2 * ROWS : 3 * ROWS]
        out_ref[q] = energy
        rho = density_ref[place_ref[q]]
        scaled = energy * (rho * rho * rho)
        for p in range(BLOCK // LANES):
            acc = acc + scaled[:, p * LANES : (p + 1) * LANES]
        return acc

    acc = lax.fori_loop(0, 4, group, jnp.zeros((ROWS, LANES), F32))
    column = jnp.sum(acc, axis=1, keepdims=True)
    row_id = lax.broadcasted_iota(jnp.int32, (ROWS, 64), 0)
    lane = lax.broadcasted_iota(jnp.int32, (ROWS, 64), 1)
    spot = jnp.where(row_id < 8, place_ref[4] * 8 + row_id, place_ref[5] * 8 + row_id - 8)
    row = jnp.sum(jnp.where(lane == spot, column, 0.0), axis=0, keepdims=True)
    parts_ref[...] = jnp.broadcast_to(row, parts_ref.shape)


def split(x):
    high = x.astype(BF16)
    return high, (x - high.astype(F32)).astype(BF16)


def send_kernel(elements, place_ref, count_ref, parts_ref, energy_ref, density_ref, picks_ref, comp_ref, out_ref):
    comp = jnp.sum(parts_ref[...], axis=0, keepdims=True) / elements
    comp_ref[...] = comp
    center = jnp.mean(comp, axis=1, keepdims=True)
    spread = jnp.sqrt(jnp.mean((comp - center) ** 2, axis=1, keepdims=True) + epsilon)
    weight = (1.0 + spread_weight * (comp - center) / spread) / 64.0
    row_id = lax.broadcasted_iota(jnp.int32, (ROWS, 64), 0)
    lane = lax.broadcasted_iota(jnp.int32, (ROWS, 64), 1)
    spot = jnp.where(row_id < 8, place_ref[4] * 8 + row_id, place_ref[5] * 8 + row_id - 8)
    column = jnp.sum(jnp.where(lane == spot, weight, 0.0), axis=1, keepdims=True)
    _, dests, width = picks_ref.shape
    low_id = lax.broadcasted_iota(jnp.int32, (LANES, width), 0)
    high_id = lax.broadcasted_iota(jnp.int32, (16, width), 0)
    slot = lax.broadcasted_iota(jnp.int32, (16, width), 1)
    for q in range(4):
        energy = energy_ref[q]
        rho = density_ref[place_ref[q]]
        sens = -penalty * rho * rho * jnp.sum(column * energy, axis=0, keepdims=True)
        mean = jnp.sum(energy, axis=0, keepdims=True) / 64.0
        both = [f[:, h * LANES : (h + 1) * LANES] for f in (sens, mean) for h in range(16)]
        table = jnp.concatenate(split(jnp.concatenate(both, axis=0)), axis=0)
        for d in range(dests):
            pick = picks_ref[q, d : d + 1, :]
            hot = jnp.where(low_id == (pick & (LANES - 1)), 1.0, 0.0).astype(BF16)
            found = jnp.dot(table, hot, preferred_element_type=F32)
            found = found[:32] + found[32:]
            live = (high_id == (pick >> 7)) & (slot < count_ref[place_ref[q] * 16 + d])
            for f in range(2):
                got = jnp.sum(jnp.where(live, found[16 * f : 16 * f + 16], 0.0), axis=0, keepdims=True)
                for p in range(width // LANES):
                    r = f * (width // LANES) + p
                    out_ref[q * dests + d, r : r + 1, :] = got[:, p * LANES : (p + 1) * LANES]


def owner_kernel(got_ref, cells_ref, filter_ref, sens_ref, energy_ref):
    sources, width = cells_ref.shape[2], cells_ref.shape[3]
    low_id = lax.broadcasted_iota(jnp.int32, (LANES, width), 0)
    high_id = lax.broadcasted_iota(jnp.int32, (16, width), 0)
    node = jnp.zeros((64, LANES), F32)
    for j in range(sources):
        cell = cells_ref[0, 0, j : j + 1, :]
        hot = jnp.where(low_id == (cell & (LANES - 1)), 1.0, 0.0).astype(BF16)
        mine = high_id == (cell >> 7)
        pieces = []
        share = got_ref[j]
        for q in range(1, 4):
            share = share + got_ref[q * sources + j]
        for f in range(2):
            value = jnp.concatenate([share[2 * f : 2 * f + 1], share[2 * f + 1 : 2 * f + 2]], axis=1)
            pieces.append(jnp.where(mine, value, 0.0))
        rows = jnp.concatenate(split(jnp.concatenate(pieces, axis=0)), axis=0)
        node = node + lax.dot_general(rows, hot, (((1,), (1,)), ((), ())), preferred_element_type=F32)
    node = node[:32] + node[32:]
    result = lax.dot_general(
        node, filter_ref[...], (((1,), (1,)), ((), ())),
        precision=lax.Precision.HIGHEST, preferred_element_type=F32,
    )
    for p in range(16):
        sens_ref[0, :, p * LANES : (p + 1) * LANES] = result[p : p + 1]
        energy_ref[0, :, p * LANES : (p + 1) * LANES] = result[16 + p : 17 + p]


def block_stiffness(stiffness):
    lane = jnp.arange(512, dtype=jnp.int32)
    spot = lane % 64
    corner = 2 * (lane // LANES) + (lane % LANES) // 64
    dof = jnp.where(spot < 48, 8 * (spot // ROWS) + corner, -1)
    hot = (dof[:, None] == jnp.arange(24, dtype=jnp.int32)[None, :]).astype(BF16)
    wide = jnp.dot(hot, jnp.dot(stiffness.T, hot.T, preferred_element_type=F32).astype(BF16), preferred_element_type=F32)
    same = (lane % ROWS)[:, None] == (lane % ROWS)[None, :]
    return jnp.where(same, wide, 0.0).astype(BF16)


def body(displacements, connectivity, density, stiffness, filter_inverse, send_rows, send_count, recv_cell):
    group_id = lax.axis_index("sample")
    core = group_id % 2
    node_count = displacements.shape[2]
    elements = density.shape[0]
    groups = 8
    sub_rows = elements // groups
    slabs = lax.axis_size("space")
    nodes = (node_count + LANES - 1) // LANES * LANES

    own = jnp.transpose(displacements, (1, 0, 2)).reshape(24, node_count).astype(F32)
    own = jnp.pad(own, ((0, 0), (0, nodes - node_count)))
    other = lax.ppermute(own, "sample", [(i, i ^ 1) for i in range(8)])
    links = connectivity.reshape(-1)
    rho = density.reshape(groups, 1, sub_rows)
    weights = block_stiffness(stiffness)

    place = jnp.stack([2 * q + core for q in range(4)] + [group_id, group_id ^ 1]).astype(jnp.int32)
    whole = pl.BlockSpec(memory_space=pltpu.VMEM)
    smem = pl.BlockSpec(memory_space=pltpu.SMEM)
    energies, mine = pl.pallas_call(
        energy_kernel,
        in_specs=[smem, pl.BlockSpec(memory_space=pl.ANY)] + [whole] * 4,
        out_specs=[whole] * 2,
        out_shape=[jax.ShapeDtypeStruct((4, ROWS, sub_rows), F32), jax.ShapeDtypeStruct((128, 64), F32)],
        scratch_shapes=[pltpu.VMEM((nodes, LANES), F32), pltpu.VMEM((BLOCK, 4 * LANES), F32)]
        + [pltpu.SMEM((4 * BLOCK,), jnp.int32)] * 8
        + [pltpu.SemaphoreType.DMA((8, 4))],
        compiler_params=pltpu.CompilerParams(vmem_limit_bytes=30 * 2**20),
        name="energy",
    )(place, links, own, other, weights, rho)
    parts = lax.all_to_all(mine, ("sample", "space"), split_axis=0, concat_axis=0, tiled=True)
    dests, width = send_rows.shape[-2:]
    picks = lax.dynamic_index_in_dim(send_rows.reshape(4, 2, dests, width), core, 1, keepdims=False)
    compliance, outgoing = pl.pallas_call(
        functools.partial(send_kernel, float(elements * slabs)),
        in_specs=[smem, smem] + [whole] * 4,
        out_specs=[whole] * 2,
        out_shape=[
            jax.ShapeDtypeStruct((1, 64), F32),
            jax.ShapeDtypeStruct((4 * dests, 2 * width // LANES, LANES), F32),
        ],
        compiler_params=pltpu.CompilerParams(vmem_limit_bytes=8 * 2**20),
        name="send",
    )(place, send_count.reshape(-1), parts, energies, rho, picks)
    peers = [[i * slabs + j for i in range(c, groups, 2) for j in range(slabs)] for c in range(2)]
    got = lax.all_to_all(
        outgoing, ("sample", "space"), split_axis=0, concat_axis=0, tiled=True, axis_index_groups=peers
    )
    sens, energy = pl.pallas_call(
        owner_kernel,
        in_specs=[whole] * 3,
        out_specs=[whole] * 2,
        out_shape=[jax.ShapeDtypeStruct((1, 1, sub_rows), F32)] * 2,
        compiler_params=pltpu.CompilerParams(vmem_limit_bytes=8 * 2**20),
        name="owner",
    )(got, recv_cell, filter_inverse)
    return (compliance.reshape(-1), sens, energy)


def solution(mesh):
    in_specs = (
        P("sample", None, "space"),
        P(None, "space"),
        P("space"),
        P(),
        P(),
        P("space", None, None, None),
        P("space", None, None),
        P("sample", "space", None, None),
    )
    out_specs = (P(), P("sample", "space", None), P("sample", "space", None))
    return jax.shard_map(body, mesh=mesh, in_specs=in_specs, out_specs=out_specs, check_vma=False)
```

```python
import functools

import jax
import jax.numpy as jnp
from jax import lax
from jax.experimental import pallas as pl
from jax.experimental.pallas import tpu as pltpu
from jax.sharding import PartitionSpec as P

penalty = 3.0
spread_weight = 0.5
epsilon = 1e-06

LANES = 128
BLOCK = 2048
FILL = 29
UNROLL = 128
ROWS = 16
F32 = jnp.float32
BF16 = jnp.bfloat16


def energy_kernel(place_ref, links_ref, own_ref, other_ref, weight_ref, density_ref, out_ref, parts_ref, table, rows, *rest):
    links, sem = rest[:8], rest[8]
    elements = links_ref.shape[0] // 8

    def link_copy(c, q):
        start = pl.multiple_of(c * elements + place_ref[q] * BLOCK, BLOCK)
        there = links[c].at[pl.ds(pl.multiple_of(q * BLOCK, BLOCK), BLOCK)]
        return pltpu.make_async_copy(links_ref.at[pl.ds(start, BLOCK)], there, sem.at[c, q])

    for q in range(4):
        for c in range(8):
            link_copy(c, q).start()

    row = lax.broadcasted_iota(jnp.int32, (LANES // 2, LANES), 0)
    lane = lax.broadcasted_iota(jnp.int32, (LANES // 2, LANES), 1)
    twice = jnp.where(row == lane % (LANES // 2), 1.0, 0.0).astype(BF16)

    def fill(n, _):
        at = pl.ds(pl.multiple_of(n * (FILL * LANES), LANES), FILL * LANES)
        own, other = own_ref[:, at], other_ref[:, at]
        half = []
        for k in range(3):
            half += [own[8 * k : 8 * k + 8], other[8 * k : 8 * k + 8]]
        half = jnp.concatenate(half + [jnp.zeros((ROWS, FILL * LANES), F32)], axis=0).astype(BF16)
        table[at, :] = lax.dot_general(half, twice, (((0,), (0,)), ((), ())), preferred_element_type=F32)
        return 0

    lax.fori_loop(0, table.shape[0] // (FILL * LANES), fill, 0)

    first_half = lax.broadcasted_iota(jnp.int32, (1, LANES), 1) < LANES // 2
    reach = 4 * BLOCK - UNROLL

    def group(q, acc):
        for c in range(8):
            link_copy(c, q).wait()

        def gather(t, _):
            start = pl.multiple_of(t * UNROLL, UNROLL)
            view = rows.at[pl.ds(start, UNROLL)]
            e = q * BLOCK + start
            for u in range(UNROLL):
                for p in range(4):
                    low = table[pl.ds(links[2 * p].at[pl.ds(u, reach)][e], 1), :]
                    high = table[pl.ds(links[2 * p + 1].at[pl.ds(u, reach)][e], 1), :]
                    view[u : u + 1, p * LANES : (p + 1) * LANES] = jnp.where(first_half, low, high)
            return 0

        lax.fori_loop(0, BLOCK // UNROLL, gather, 0)
        field = rows[...]
        applied = jnp.dot(field.astype(BF16), weight_ref[...], preferred_element_type=F32)
        product = field * applied
        folded = product[:, :LANES]
        for p in range(1, 4):
            folded = folded + product[:, p * LANES : (p + 1) * LANES]
        turned = folded.T
        half = turned[: LANES // 2] + turned[LANES // 2 :]
        energy = half[:ROWS] + half[ROWS : 2 * ROWS] + half[2 * ROWS : 3 * ROWS]
        out_ref[q] = energy
        rho = density_ref[place_ref[q]]
        scaled = energy * (rho * rho * rho)
        for p in range(BLOCK // LANES):
            acc = acc + scaled[:, p * LANES : (p + 1) * LANES]
        return acc

    acc = lax.fori_loop(0, 4, group, jnp.zeros((ROWS, LANES), F32))
    column = jnp.sum(acc, axis=1, keepdims=True)
    row_id = lax.broadcasted_iota(jnp.int32, (ROWS, 64), 0)
    lane = lax.broadcasted_iota(jnp.int32, (ROWS, 64), 1)
    spot = jnp.where(row_id < 8, place_ref[4] * 8 + row_id, place_ref[5] * 8 + row_id - 8)
    row = jnp.sum(jnp.where(lane == spot, column, 0.0), axis=0, keepdims=True)
    parts_ref[...] = jnp.broadcast_to(row, parts_ref.shape)


def split(x):
    high = x.astype(BF16)
    return high, (x - high.astype(F32)).astype(BF16)


def prepare_kernel(cells_ref, filter_in, _, hot_ref, mine_ref, filter_ref):
    filter_ref[...] = filter_in[...]
    sources, width = cells_ref.shape[2:]
    low_id = lax.broadcasted_iota(jnp.int32, (LANES, width), 0)
    high_id = lax.broadcasted_iota(jnp.int32, (16, width), 0)
    for j in range(sources):
        cell = cells_ref[0, 0, j : j + 1, :]
        hot_ref[j] = jnp.where(low_id == (cell & (LANES - 1)), 1.0, 0.0).astype(BF16)
        mine_ref[j] = jnp.where(high_id == (cell >> 7), 1.0, 0.0)


def send_kernel(elements, place_ref, count_ref, parts_ref, energy_ref, density_ref, picks_ref, comp_ref, out_ref):
    comp = jnp.sum(parts_ref[...], axis=0, keepdims=True) / elements
    comp_ref[...] = comp
    center = jnp.mean(comp, axis=1, keepdims=True)
    spread = jnp.sqrt(jnp.mean((comp - center) ** 2, axis=1, keepdims=True) + epsilon)
    weight = (1.0 + spread_weight * (comp - center) / spread) / 64.0
    row_id = lax.broadcasted_iota(jnp.int32, (ROWS, 64), 0)
    lane = lax.broadcasted_iota(jnp.int32, (ROWS, 64), 1)
    spot = jnp.where(row_id < 8, place_ref[4] * 8 + row_id, place_ref[5] * 8 + row_id - 8)
    column = jnp.sum(jnp.where(lane == spot, weight, 0.0), axis=1, keepdims=True)
    _, dests, width = picks_ref.shape
    low_id = lax.broadcasted_iota(jnp.int32, (LANES, width), 0)
    high_id = lax.broadcasted_iota(jnp.int32, (16, width), 0)
    slot = lax.broadcasted_iota(jnp.int32, (16, width), 1)
    for q in range(4):
        energy = energy_ref[q]
        rho = density_ref[place_ref[q]]
        sens = -penalty * rho * rho * jnp.sum(column * energy, axis=0, keepdims=True)
        mean = jnp.sum(energy, axis=0, keepdims=True) / 64.0
        both = [f[:, h * LANES : (h + 1) * LANES] for f in (sens, mean) for h in range(16)]
        table = jnp.concatenate(split(jnp.concatenate(both, axis=0)), axis=0)
        for d in range(dests):
            pick = picks_ref[q, d : d + 1, :]
            hot = jnp.where(low_id == (pick & (LANES - 1)), 1.0, 0.0).astype(BF16)
            found = jnp.dot(table, hot, preferred_element_type=F32)
            found = found[:32] + found[32:]
            live = (high_id == (pick >> 7)) & (slot < count_ref[place_ref[q] * 16 + d])
            for f in range(2):
                got = jnp.sum(jnp.where(live, found[16 * f : 16 * f + 16], 0.0), axis=0, keepdims=True)
                for p in range(width // LANES):
                    r = f * (width // LANES) + p
                    out_ref[q * dests + d, r : r + 1, :] = got[:, p * LANES : (p + 1) * LANES]


def owner_kernel(got_ref, hot_ref, mine_ref, filter_ref, sens_ref, energy_ref):
    sources = hot_ref.shape[0]
    node = jnp.zeros((64, LANES), F32)
    for j in range(sources):
        pieces = []
        share = got_ref[j]
        for q in range(1, 4):
            share = share + got_ref[q * sources + j]
        for f in range(2):
            value = jnp.concatenate([share[2 * f : 2 * f + 1], share[2 * f + 1 : 2 * f + 2]], axis=1)
            pieces.append(mine_ref[j] * value)
        rows = jnp.concatenate(split(jnp.concatenate(pieces, axis=0)), axis=0)
        node = node + lax.dot_general(rows, hot_ref[j], (((1,), (1,)), ((), ())), preferred_element_type=F32)
    node = node[:32] + node[32:]
    result = lax.dot_general(
        node, filter_ref[...], (((1,), (1,)), ((), ())),
        precision=lax.Precision.HIGHEST, preferred_element_type=F32,
    )
    for p in range(16):
        sens_ref[0, :, p * LANES : (p + 1) * LANES] = result[p : p + 1]
        energy_ref[0, :, p * LANES : (p + 1) * LANES] = result[16 + p : 17 + p]


def block_stiffness(stiffness):
    lane = jnp.arange(512, dtype=jnp.int32)
    spot = lane % 64
    corner = 2 * (lane // LANES) + (lane % LANES) // 64
    dof = jnp.where(spot < 48, 8 * (spot // ROWS) + corner, -1)
    hot = (dof[:, None] == jnp.arange(24, dtype=jnp.int32)[None, :]).astype(BF16)
    wide = jnp.dot(hot, jnp.dot(stiffness.T, hot.T, preferred_element_type=F32).astype(BF16), preferred_element_type=F32)
    same = (lane % ROWS)[:, None] == (lane % ROWS)[None, :]
    return jnp.where(same, wide, 0.0).astype(BF16)


def body(displacements, connectivity, density, stiffness, filter_inverse, send_rows, send_count, recv_cell):
    group_id = lax.axis_index("sample")
    core = group_id % 2
    node_count = displacements.shape[2]
    elements = density.shape[0]
    groups = 8
    sub_rows = elements // groups
    slabs = lax.axis_size("space")
    nodes = (node_count + LANES - 1) // LANES * LANES

    own = jnp.transpose(displacements, (1, 0, 2)).reshape(24, node_count).astype(F32)
    own = jnp.pad(own, ((0, 0), (0, nodes - node_count)))
    other = lax.ppermute(own, "sample", [(i, i ^ 1) for i in range(8)])
    links = connectivity.reshape(-1)
    rho = density.reshape(groups, 1, sub_rows)
    weights = block_stiffness(stiffness)

    place = jnp.stack([2 * q + core for q in range(4)] + [group_id, group_id ^ 1]).astype(jnp.int32)
    whole = pl.BlockSpec(memory_space=pltpu.VMEM)
    smem = pl.BlockSpec(memory_space=pltpu.SMEM)
    energies, mine = pl.pallas_call(
        energy_kernel,
        in_specs=[smem, pl.BlockSpec(memory_space=pl.ANY)] + [whole] * 4,
        out_specs=[whole] * 2,
        out_shape=[jax.ShapeDtypeStruct((4, ROWS, sub_rows), F32), jax.ShapeDtypeStruct((128, 64), F32)],
        scratch_shapes=[pltpu.VMEM((nodes, LANES), F32), pltpu.VMEM((BLOCK, 4 * LANES), F32)]
        + [pltpu.SMEM((4 * BLOCK,), jnp.int32)] * 8
        + [pltpu.SemaphoreType.DMA((8, 4))],
        compiler_params=pltpu.CompilerParams(vmem_limit_bytes=30 * 2**20),
        name="energy",
    )(place, links, own, other, weights, rho)
    parts = lax.all_to_all(mine, ("sample", "space"), split_axis=0, concat_axis=0, tiled=True)
    dests, width = send_rows.shape[-2:]
    picks = lax.dynamic_index_in_dim(send_rows.reshape(4, 2, dests, width), core, 1, keepdims=False)
    small = pltpu.CompilerParams(vmem_limit_bytes=8 * 2**20)
    cell_hot, cell_mine, near_filter = pl.pallas_call(
        prepare_kernel,
        in_specs=[whole, whole, pl.BlockSpec(memory_space=pl.ANY)],
        out_specs=[whole] * 3,
        out_shape=[
            jax.ShapeDtypeStruct((dests, LANES, width), BF16),
            jax.ShapeDtypeStruct((dests, 16, width), F32),
            jax.ShapeDtypeStruct(filter_inverse.shape, F32),
        ],
        compiler_params=small,
        cost_estimate=pl.CostEstimate(flops=4 * 10**9, bytes_accessed=2**21, transcendentals=0),
        name="prepare",
    )(recv_cell, filter_inverse, energies)
    compliance, outgoing = pl.pallas_call(
        functools.partial(send_kernel, float(elements * slabs)),
        in_specs=[smem, smem] + [whole] * 4,
        out_specs=[whole] * 2,
        out_shape=[
            jax.ShapeDtypeStruct((1, 64), F32),
            jax.ShapeDtypeStruct((4 * dests, 2 * width // LANES, LANES), F32),
        ],
        compiler_params=small,
        name="send",
    )(place, send_count.reshape(-1), parts, energies, rho, picks)
    peers = [[i * slabs + j for i in range(c, groups, 2) for j in range(slabs)] for c in range(2)]
    got = lax.all_to_all(
        outgoing, ("sample", "space"), split_axis=0, concat_axis=0, tiled=True, axis_index_groups=peers
    )
    sens, energy = pl.pallas_call(
        owner_kernel,
        in_specs=[whole] * 4,
        out_specs=[whole] * 2,
        out_shape=[jax.ShapeDtypeStruct((1, 1, sub_rows), F32)] * 2,
        compiler_params=small,
        name="owner",
    )(got, cell_hot, cell_mine, near_filter)
    return (compliance.reshape(-1), sens, energy)


def solution(mesh):
    in_specs = (
        P("sample", None, "space"),
        P(None, "space"),
        P("space"),
        P(),
        P(),
        P("space", None, None, None),
        P("space", None, None),
        P("sample", "space", None, None),
    )
    out_specs = (P(), P("sample", "space", None), P("sample", "space", None))
    return jax.shard_map(body, mesh=mesh, in_specs=in_specs, out_specs=out_specs, check_vma=False)
```

```python
import functools

import jax
import jax.numpy as jnp
from jax import lax
from jax.experimental import pallas as pl
from jax.experimental.pallas import tpu as pltpu
from jax.sharding import PartitionSpec as P

penalty = 3.0
spread_weight = 0.5
epsilon = 1e-06

LANES = 128
BLOCK = 2048
FILL = 29
UNROLL = 128
ROWS = 16
F32 = jnp.float32
BF16 = jnp.bfloat16


def energy_kernel(place_ref, links_ref, own_ref, other_ref, weight_ref, density_ref, out_ref, parts_ref, table, rows, *rest):
    links, sem = rest[:8], rest[8]
    elements = links_ref.shape[0] // 8

    def link_copy(c, q):
        start = pl.multiple_of(c * elements + place_ref[q] * BLOCK, BLOCK)
        there = links[c].at[pl.ds(pl.multiple_of(q * BLOCK, BLOCK), BLOCK)]
        return pltpu.make_async_copy(links_ref.at[pl.ds(start, BLOCK)], there, sem.at[c, q])

    for q in range(4):
        for c in range(8):
            link_copy(c, q).start()

    row = lax.broadcasted_iota(jnp.int32, (LANES // 2, LANES), 0)
    lane = lax.broadcasted_iota(jnp.int32, (LANES // 2, LANES), 1)
    twice = jnp.where(row == lane % (LANES // 2), 1.0, 0.0).astype(BF16)

    def fill(n, _):
        at = pl.ds(pl.multiple_of(n * (FILL * LANES), LANES), FILL * LANES)
        own, other = own_ref[:, at], other_ref[:, at]
        half = []
        for k in range(3):
            half += [own[8 * k : 8 * k + 8], other[8 * k : 8 * k + 8]]
        half = jnp.concatenate(half + [jnp.zeros((ROWS, FILL * LANES), F32)], axis=0).astype(BF16)
        table[at, :] = lax.dot_general(half, twice, (((0,), (0,)), ((), ())), preferred_element_type=F32)
        return 0

    lax.fori_loop(0, table.shape[0] // (FILL * LANES), fill, 0)

    first_half = lax.broadcasted_iota(jnp.int32, (1, LANES), 1) < LANES // 2
    reach = 4 * BLOCK - UNROLL

    def group(q, acc):
        for c in range(8):
            link_copy(c, q).wait()

        def gather(t, _):
            start = pl.multiple_of(t * UNROLL, UNROLL)
            view = rows.at[pl.ds(start, UNROLL)]
            e = q * BLOCK + start
            for u in range(UNROLL):
                for p in range(4):
                    low = table[pl.ds(links[2 * p].at[pl.ds(u, reach)][e], 1), :]
                    high = table[pl.ds(links[2 * p + 1].at[pl.ds(u, reach)][e], 1), :]
                    view[u : u + 1, p * LANES : (p + 1) * LANES] = jnp.where(first_half, low, high)
            return 0

        lax.fori_loop(0, BLOCK // UNROLL, gather, 0)
        field = rows[...]
        applied = jnp.dot(field.astype(BF16), weight_ref[...], preferred_element_type=F32)
        product = field * applied
        folded = product[:, :LANES]
        for p in range(1, 4):
            folded = folded + product[:, p * LANES : (p + 1) * LANES]
        turned = folded.T
        half = turned[: LANES // 2] + turned[LANES // 2 :]
        energy = half[:ROWS] + half[ROWS : 2 * ROWS] + half[2 * ROWS : 3 * ROWS]
        out_ref[q] = energy
        rho = density_ref[place_ref[q]]
        scaled = energy * (rho * rho * rho)
        for p in range(BLOCK // LANES):
            acc = acc + scaled[:, p * LANES : (p + 1) * LANES]
        return acc

    acc = lax.fori_loop(0, 4, group, jnp.zeros((ROWS, LANES), F32))
    column = jnp.sum(acc, axis=1, keepdims=True)
    row_id = lax.broadcasted_iota(jnp.int32, (ROWS, 64), 0)
    lane = lax.broadcasted_iota(jnp.int32, (ROWS, 64), 1)
    spot = jnp.where(row_id < 8, place_ref[4] * 8 + row_id, place_ref[5] * 8 + row_id - 8)
    row = jnp.sum(jnp.where(lane == spot, column, 0.0), axis=0, keepdims=True)
    parts_ref[...] = jnp.broadcast_to(row, parts_ref.shape)


def split(x):
    high = x.astype(BF16)
    return high, (x - high.astype(F32)).astype(BF16)


def prepare_kernel(cells_ref, filter_in, _, hot_ref, mine_ref, filter_ref):
    filter_ref[...] = filter_in[...]
    sources, width = cells_ref.shape[2:]
    low_id = lax.broadcasted_iota(jnp.int32, (LANES, width), 0)
    high_id = lax.broadcasted_iota(jnp.int32, (16, width), 0)
    for j in range(sources):
        cell = cells_ref[0, 0, j : j + 1, :]
        hot_ref[j] = jnp.where(low_id == (cell & (LANES - 1)), 1.0, 0.0).astype(BF16)
        mine_ref[j] = jnp.where(high_id == (cell >> 7), 1.0, 0.0)


def send_kernel(elements, place_ref, count_ref, parts_ref, energy_ref, density_ref, picks_ref, comp_ref, out_ref):
    comp = jnp.sum(parts_ref[...], axis=0, keepdims=True) / elements
    comp_ref[...] = comp
    center = jnp.mean(comp, axis=1, keepdims=True)
    spread = jnp.sqrt(jnp.mean((comp - center) ** 2, axis=1, keepdims=True) + epsilon)
    weight = (1.0 + spread_weight * (comp - center) / spread) / 64.0
    row_id = lax.broadcasted_iota(jnp.int32, (ROWS, 64), 0)
    lane = lax.broadcasted_iota(jnp.int32, (ROWS, 64), 1)
    spot = jnp.where(row_id < 8, place_ref[4] * 8 + row_id, place_ref[5] * 8 + row_id - 8)
    column = jnp.sum(jnp.where(lane == spot, weight, 0.0), axis=1, keepdims=True)
    _, dests, width = picks_ref.shape
    low_id = lax.broadcasted_iota(jnp.int32, (LANES, width), 0).astype(jnp.int16)
    one, zero = jnp.ones((LANES, width), BF16), jnp.zeros((LANES, width), BF16)
    high_id = lax.broadcasted_iota(jnp.int32, (16, width), 0)
    slot = lax.broadcasted_iota(jnp.int32, (16, width), 1)
    for q in range(4):
        energy = energy_ref[q]
        rho = density_ref[place_ref[q]]
        sens = -penalty * rho * rho * jnp.sum(column * energy, axis=0, keepdims=True)
        mean = jnp.sum(energy, axis=0, keepdims=True) / 64.0
        both = [f[:, h * LANES : (h + 1) * LANES] for f in (sens, mean) for h in range(16)]
        table = jnp.concatenate(split(jnp.concatenate(both, axis=0)), axis=0)
        for d in range(dests):
            pick = picks_ref[q, d : d + 1, :]
            hot = jnp.where(low_id == (pick & (LANES - 1)).astype(jnp.int16), one, zero)
            found = jnp.dot(table, hot, preferred_element_type=F32)
            found = found[:32] + found[32:]
            live = (high_id == (pick >> 7)) & (slot < count_ref[place_ref[q] * 16 + d])
            for f in range(2):
                got = jnp.sum(jnp.where(live, found[16 * f : 16 * f + 16], 0.0), axis=0, keepdims=True)
                for p in range(width // LANES):
                    r = f * (width // LANES) + p
                    out_ref[q * dests + d, r : r + 1, :] = got[:, p * LANES : (p + 1) * LANES]


def owner_kernel(got_ref, hot_ref, mine_ref, filter_ref, sens_ref, energy_ref):
    sources = hot_ref.shape[0]
    node = jnp.zeros((64, LANES), F32)
    for j in range(sources):
        pieces = []
        share = got_ref[j]
        for q in range(1, 4):
            share = share + got_ref[q * sources + j]
        for f in range(2):
            value = jnp.concatenate([share[2 * f : 2 * f + 1], share[2 * f + 1 : 2 * f + 2]], axis=1)
            pieces.append(mine_ref[j] * value)
        rows = jnp.concatenate(split(jnp.concatenate(pieces, axis=0)), axis=0)
        node = node + lax.dot_general(rows, hot_ref[j], (((1,), (1,)), ((), ())), preferred_element_type=F32)
    node = node[:32] + node[32:]
    result = lax.dot_general(
        node, filter_ref[...], (((1,), (1,)), ((), ())),
        precision=lax.Precision.HIGHEST, preferred_element_type=F32,
    )
    for p in range(16):
        sens_ref[0, :, p * LANES : (p + 1) * LANES] = result[p : p + 1]
        energy_ref[0, :, p * LANES : (p + 1) * LANES] = result[16 + p : 17 + p]


def block_stiffness(stiffness):
    lane = jnp.arange(512, dtype=jnp.int32)
    spot = lane % 64
    corner = 2 * (lane // LANES) + (lane % LANES) // 64
    dof = jnp.where(spot < 48, 8 * (spot // ROWS) + corner, -1)
    hot = (dof[:, None] == jnp.arange(24, dtype=jnp.int32)[None, :]).astype(BF16)
    wide = jnp.dot(hot, jnp.dot(stiffness.T, hot.T, preferred_element_type=F32).astype(BF16), preferred_element_type=F32)
    same = (lane % ROWS)[:, None] == (lane % ROWS)[None, :]
    return jnp.where(same, wide, 0.0).astype(BF16)


def body(displacements, connectivity, density, stiffness, filter_inverse, send_rows, send_count, recv_cell):
    group_id = lax.axis_index("sample")
    core = group_id % 2
    node_count = displacements.shape[2]
    elements = density.shape[0]
    groups = 8
    sub_rows = elements // groups
    slabs = lax.axis_size("space")
    nodes = (node_count + LANES - 1) // LANES * LANES

    own = jnp.transpose(displacements, (1, 0, 2)).reshape(24, node_count).astype(F32)
    own = jnp.pad(own, ((0, 0), (0, nodes - node_count)))
    other = lax.ppermute(own, "sample", [(i, i ^ 1) for i in range(8)])
    links = connectivity.reshape(-1)
    rho = density.reshape(groups, 1, sub_rows)
    weights = block_stiffness(stiffness)

    place = jnp.stack([2 * q + core for q in range(4)] + [group_id, group_id ^ 1]).astype(jnp.int32)
    whole = pl.BlockSpec(memory_space=pltpu.VMEM)
    smem = pl.BlockSpec(memory_space=pltpu.SMEM)
    energies, mine = pl.pallas_call(
        energy_kernel,
        in_specs=[smem, pl.BlockSpec(memory_space=pl.ANY)] + [whole] * 4,
        out_specs=[whole] * 2,
        out_shape=[jax.ShapeDtypeStruct((4, ROWS, sub_rows), F32), jax.ShapeDtypeStruct((128, 64), F32)],
        scratch_shapes=[pltpu.VMEM((nodes, LANES), F32), pltpu.VMEM((BLOCK, 4 * LANES), F32)]
        + [pltpu.SMEM((4 * BLOCK,), jnp.int32)] * 8
        + [pltpu.SemaphoreType.DMA((8, 4))],
        compiler_params=pltpu.CompilerParams(vmem_limit_bytes=30 * 2**20),
        name="energy",
    )(place, links, own, other, weights, rho)
    parts = lax.all_to_all(mine, ("sample", "space"), split_axis=0, concat_axis=0, tiled=True)
    dests, width = send_rows.shape[-2:]
    picks = lax.dynamic_index_in_dim(send_rows.reshape(4, 2, dests, width), core, 1, keepdims=False)
    small = pltpu.CompilerParams(vmem_limit_bytes=8 * 2**20)
    cell_hot, cell_mine, near_filter = pl.pallas_call(
        prepare_kernel,
        in_specs=[whole, whole, pl.BlockSpec(memory_space=pl.ANY)],
        out_specs=[whole] * 3,
        out_shape=[
            jax.ShapeDtypeStruct((dests, LANES, width), BF16),
            jax.ShapeDtypeStruct((dests, 16, width), F32),
            jax.ShapeDtypeStruct(filter_inverse.shape, F32),
        ],
        compiler_params=small,
        cost_estimate=pl.CostEstimate(flops=4 * 10**9, bytes_accessed=2**21, transcendentals=0),
        name="prepare",
    )(recv_cell, filter_inverse, energies)
    compliance, outgoing = pl.pallas_call(
        functools.partial(send_kernel, float(elements * slabs)),
        in_specs=[smem, smem] + [whole] * 4,
        out_specs=[whole] * 2,
        out_shape=[
            jax.ShapeDtypeStruct((1, 64), F32),
            jax.ShapeDtypeStruct((4 * dests, 2 * width // LANES, LANES), F32),
        ],
        compiler_params=small,
        name="send",
    )(place, send_count.reshape(-1), parts, energies, rho, picks)
    peers = [[i * slabs + j for i in range(c, groups, 2) for j in range(slabs)] for c in range(2)]
    got = lax.all_to_all(
        outgoing, ("sample", "space"), split_axis=0, concat_axis=0, tiled=True, axis_index_groups=peers
    )
    sens, energy = pl.pallas_call(
        owner_kernel,
        in_specs=[whole] * 4,
        out_specs=[whole] * 2,
        out_shape=[jax.ShapeDtypeStruct((1, 1, sub_rows), F32)] * 2,
        compiler_params=small,
        name="owner",
    )(got, cell_hot, cell_mine, near_filter)
    return (compliance.reshape(-1), sens, energy)


def solution(mesh):
    in_specs = (
        P("sample", None, "space"),
        P(None, "space"),
        P("space"),
        P(),
        P(),
        P("space", None, None, None),
        P("space", None, None),
        P("sample", "space", None, None),
    )
    out_specs = (P(), P("sample", "space", None), P("sample", "space", None))
    return jax.shard_map(body, mesh=mesh, in_specs=in_specs, out_specs=out_specs, check_vma=False)
```

```python
import functools

import jax
import jax.numpy as jnp
from jax import lax
from jax.experimental import pallas as pl
from jax.experimental.pallas import tpu as pltpu
from jax.sharding import PartitionSpec as P

penalty = 3.0
spread_weight = 0.5
epsilon = 1e-06

LANES = 128
BLOCK = 2048
FILL = 29
UNROLL = 128
ROWS = 16
F32 = jnp.float32
BF16 = jnp.bfloat16


def energy_kernel(place_ref, links_ref, own_ref, other_ref, weight_ref, density_ref, out_ref, parts_ref, table, rows, *rest):
    links, sem = rest[:8], rest[8]
    elements = links_ref.shape[0] // 8

    def link_copy(c, q):
        start = pl.multiple_of(c * elements + place_ref[q] * BLOCK, BLOCK)
        there = links[c].at[pl.ds(pl.multiple_of(q * BLOCK, BLOCK), BLOCK)]
        return pltpu.make_async_copy(links_ref.at[pl.ds(start, BLOCK)], there, sem.at[c, q])

    for q in range(4):
        for c in range(8):
            link_copy(c, q).start()

    row = lax.broadcasted_iota(jnp.int32, (LANES // 2, LANES), 0)
    lane = lax.broadcasted_iota(jnp.int32, (LANES // 2, LANES), 1)
    twice = jnp.where(row == lane % (LANES // 2), 1.0, 0.0).astype(BF16)

    def fill(n, _):
        at = pl.ds(pl.multiple_of(n * (FILL * LANES), LANES), FILL * LANES)
        own, other = own_ref[:, at], other_ref[:, at]
        half = []
        for k in range(3):
            half += [own[8 * k : 8 * k + 8], other[8 * k : 8 * k + 8]]
        half = jnp.concatenate(half + [jnp.zeros((ROWS, FILL * LANES), F32)], axis=0).astype(BF16)
        table[at, :] = lax.dot_general(half, twice, (((0,), (0,)), ((), ())), preferred_element_type=F32)
        return 0

    lax.fori_loop(0, table.shape[0] // (FILL * LANES), fill, 0)

    first_half = lax.broadcasted_iota(jnp.int32, (1, LANES), 1) < LANES // 2
    reach = 4 * BLOCK - UNROLL

    def group(q, acc):
        for c in range(8):
            link_copy(c, q).wait()

        def gather(t, _):
            start = pl.multiple_of(t * UNROLL, UNROLL)
            view = rows.at[pl.ds(start, UNROLL)]
            e = q * BLOCK + start
            for u in range(UNROLL):
                for p in range(4):
                    low = table[pl.ds(links[2 * p].at[pl.ds(u, reach)][e], 1), :]
                    high = table[pl.ds(links[2 * p + 1].at[pl.ds(u, reach)][e], 1), :]
                    view[u : u + 1, p * LANES : (p + 1) * LANES] = jnp.where(first_half, low, high)
            return 0

        lax.fori_loop(0, BLOCK // UNROLL, gather, 0)
        field = rows[...]
        applied = jnp.dot(field.astype(BF16), weight_ref[...], preferred_element_type=F32)
        product = field * applied
        folded = product[:, :LANES]
        for p in range(1, 4):
            folded = folded + product[:, p * LANES : (p + 1) * LANES]
        turned = folded.T
        half = turned[: LANES // 2] + turned[LANES // 2 :]
        energy = half[:ROWS] + half[ROWS : 2 * ROWS] + half[2 * ROWS : 3 * ROWS]
        out_ref[q] = energy
        rho = density_ref[place_ref[q]]
        scaled = energy * (rho * rho * rho)
        for p in range(BLOCK // LANES):
            acc = acc + scaled[:, p * LANES : (p + 1) * LANES]
        return acc

    acc = lax.fori_loop(0, 4, group, jnp.zeros((ROWS, LANES), F32))
    column = jnp.sum(acc, axis=1, keepdims=True)
    row_id = lax.broadcasted_iota(jnp.int32, (ROWS, 64), 0)
    lane = lax.broadcasted_iota(jnp.int32, (ROWS, 64), 1)
    spot = jnp.where(row_id < 8, place_ref[4] * 8 + row_id, place_ref[5] * 8 + row_id - 8)
    row = jnp.sum(jnp.where(lane == spot, column, 0.0), axis=0, keepdims=True)
    parts_ref[...] = jnp.broadcast_to(row, parts_ref.shape)


def split(x):
    high = x.astype(BF16)
    return high, (x - high.astype(F32)).astype(BF16)


def prepare_kernel(cells_ref, filter_in, _, hot_ref, mine_ref, filter_ref):
    filter_ref[...] = filter_in[...]
    sources, width = cells_ref.shape[2:]
    low_id = lax.broadcasted_iota(jnp.int32, (LANES, width), 0)
    high_id = lax.broadcasted_iota(jnp.int32, (16, width), 0)
    for j in range(sources):
        cell = cells_ref[0, 0, j : j + 1, :]
        hot_ref[j] = jnp.where(low_id == (cell & (LANES - 1)), 1.0, 0.0).astype(BF16)
        mine_ref[j] = jnp.where(high_id == (cell >> 7), 1.0, 0.0)


def send_kernel(elements, place_ref, count_ref, parts_ref, energy_ref, density_ref, picks_ref, out_ref):
    comp = jnp.sum(parts_ref[...], axis=0, keepdims=True) / elements
    lane = lax.broadcasted_iota(jnp.int32, (1, 64), 1)
    near = jnp.sum(comp, axis=1, keepdims=True) / ROWS
    away = jnp.where((lane >> 4) == (place_ref[4] >> 1), comp - near, 0.0)
    scale = jnp.max(jnp.abs(away), axis=1, keepdims=True)
    away = away / jnp.maximum(scale, 1e-30)
    row_id = lax.broadcasted_iota(jnp.int32, (ROWS, 64), 0)
    lanes = lax.broadcasted_iota(jnp.int32, (ROWS, 64), 1)
    spot = jnp.where(row_id < 8, place_ref[4] * 8 + row_id, place_ref[5] * 8 + row_id - 8)
    column = jnp.sum(jnp.where(lanes == spot, away, 0.0), axis=1, keepdims=True)
    comp = jnp.concatenate([comp, jnp.zeros_like(comp)], axis=1)
    wide = lax.broadcasted_iota(jnp.int32, (1, LANES), 1)
    facts = jnp.concatenate([comp, jnp.where(wide < 64, near, scale)], axis=0)
    _, dests, width = picks_ref.shape
    low_id = lax.broadcasted_iota(jnp.int32, (LANES, width), 0).astype(jnp.int16)
    one, zero = jnp.ones((LANES, width), BF16), jnp.zeros((LANES, width), BF16)
    high_id = lax.broadcasted_iota(jnp.int32, (16, width), 0)
    slot = lax.broadcasted_iota(jnp.int32, (16, width), 1)
    for q in range(4):
        energy = energy_ref[q]
        rho = density_ref[place_ref[q]]
        total = jnp.sum(energy, axis=0, keepdims=True) / 64.0
        tilted = jnp.sum(column * energy, axis=0, keepdims=True) / 64.0
        slope = -penalty * rho * rho
        both = [f[:, h * LANES : (h + 1) * LANES] for f in (slope * total, slope * tilted, total) for h in range(16)]
        table = jnp.concatenate(split(jnp.concatenate(both, axis=0)), axis=0)
        for d in range(dests):
            pick = picks_ref[q, d : d + 1, :]
            hot = jnp.where(low_id == (pick & (LANES - 1)).astype(jnp.int16), one, zero)
            found = jnp.dot(table, hot, preferred_element_type=F32)
            found = found[:48] + found[48:]
            live = (high_id == (pick >> 7)) & (slot < count_ref[place_ref[q] * 16 + d])
            for f in range(3):
                got = jnp.sum(jnp.where(live, found[16 * f : 16 * f + 16], 0.0), axis=0, keepdims=True)
                for p in range(width // LANES):
                    r = f * (width // LANES) + p
                    out_ref[q * dests + d, r : r + 1, :] = got[:, p * LANES : (p + 1) * LANES]
            out_ref[q * dests + d, 6:8, :] = facts


def owner_kernel(got_ref, hot_ref, mine_ref, filter_ref, comp_ref, sens_ref, energy_ref):
    sources = hot_ref.shape[0]
    facts = [got_ref[q * sources, 6:8, :] for q in range(4)]
    comp = (facts[0] + facts[1] + facts[2] + facts[3])[:1, :64]
    comp_ref[...] = comp
    center = jnp.mean(comp, axis=1, keepdims=True)
    spread = jnp.sqrt(jnp.mean((comp - center) ** 2, axis=1, keepdims=True) + epsilon)
    row_id = lax.broadcasted_iota(jnp.int32, (8, LANES), 0)
    factors = []
    for q in range(4):
        near, scale = facts[q][1:2, :1], facts[q][1:2, 64:65]
        plain = 1.0 + spread_weight * (near - center) / spread
        factors.append(jnp.where(row_id < 2, plain, jnp.where(row_id < 4, spread_weight * (scale / spread), 1.0)))
    node = jnp.zeros((64, LANES), F32)
    for j in range(sources):
        share = factors[0] * got_ref[j]
        for q in range(1, 4):
            share = share + factors[q] * got_ref[q * sources + j]
        pieces = []
        for value in (share[0:2] + share[2:4], share[4:6]):
            value = jnp.concatenate([value[0:1], value[1:2]], axis=1)
            pieces.append(mine_ref[j] * value)
        rows = jnp.concatenate(split(jnp.concatenate(pieces, axis=0)), axis=0)
        node = node + lax.dot_general(rows, hot_ref[j], (((1,), (1,)), ((), ())), preferred_element_type=F32)
    node = node[:32] + node[32:]
    result = lax.dot_general(
        node, filter_ref[...], (((1,), (1,)), ((), ())),
        precision=lax.Precision.HIGHEST, preferred_element_type=F32,
    )
    for p in range(16):
        sens_ref[0, :, p * LANES : (p + 1) * LANES] = result[p : p + 1]
        energy_ref[0, :, p * LANES : (p + 1) * LANES] = result[16 + p : 17 + p]


def block_stiffness(stiffness):
    lane = jnp.arange(512, dtype=jnp.int32)
    spot = lane % 64
    corner = 2 * (lane // LANES) + (lane % LANES) // 64
    dof = jnp.where(spot < 48, 8 * (spot // ROWS) + corner, -1)
    hot = (dof[:, None] == jnp.arange(24, dtype=jnp.int32)[None, :]).astype(BF16)
    wide = jnp.dot(hot, jnp.dot(stiffness.T, hot.T, preferred_element_type=F32).astype(BF16), preferred_element_type=F32)
    same = (lane % ROWS)[:, None] == (lane % ROWS)[None, :]
    return jnp.where(same, wide, 0.0).astype(BF16)


def body(displacements, connectivity, density, stiffness, filter_inverse, send_rows, send_count, recv_cell):
    group_id = lax.axis_index("sample")
    core = group_id % 2
    node_count = displacements.shape[2]
    elements = density.shape[0]
    groups = 8
    sub_rows = elements // groups
    slabs = lax.axis_size("space")
    nodes = (node_count + LANES - 1) // LANES * LANES

    own = jnp.transpose(displacements, (1, 0, 2)).reshape(24, node_count).astype(F32)
    own = jnp.pad(own, ((0, 0), (0, nodes - node_count)))
    other = lax.ppermute(own, "sample", [(i, i ^ 1) for i in range(8)])
    links = connectivity.reshape(-1)
    rho = density.reshape(groups, 1, sub_rows)
    weights = block_stiffness(stiffness)

    place = jnp.stack([2 * q + core for q in range(4)] + [group_id, group_id ^ 1]).astype(jnp.int32)
    whole = pl.BlockSpec(memory_space=pltpu.VMEM)
    smem = pl.BlockSpec(memory_space=pltpu.SMEM)
    energies, mine = pl.pallas_call(
        energy_kernel,
        in_specs=[smem, pl.BlockSpec(memory_space=pl.ANY)] + [whole] * 4,
        out_specs=[whole] * 2,
        out_shape=[jax.ShapeDtypeStruct((4, ROWS, sub_rows), F32), jax.ShapeDtypeStruct((2 * slabs, 64), F32)],
        scratch_shapes=[pltpu.VMEM((nodes, LANES), F32), pltpu.VMEM((BLOCK, 4 * LANES), F32)]
        + [pltpu.SMEM((4 * BLOCK,), jnp.int32)] * 8
        + [pltpu.SemaphoreType.DMA((8, 4))],
        compiler_params=pltpu.CompilerParams(vmem_limit_bytes=30 * 2**20),
        name="energy",
    )(place, links, own, other, weights, rho)
    chips = [[i * slabs + j for i in (c, c + 1) for j in range(slabs)] for c in range(0, groups, 2)]
    parts = lax.all_to_all(mine, ("sample", "space"), split_axis=0, concat_axis=0, tiled=True, axis_index_groups=chips)
    dests, width = send_rows.shape[-2:]
    picks = lax.dynamic_index_in_dim(send_rows.reshape(4, 2, dests, width), core, 1, keepdims=False)
    small = pltpu.CompilerParams(vmem_limit_bytes=8 * 2**20)
    cell_hot, cell_mine, near_filter = pl.pallas_call(
        prepare_kernel,
        in_specs=[whole, whole, pl.BlockSpec(memory_space=pl.ANY)],
        out_specs=[whole] * 3,
        out_shape=[
            jax.ShapeDtypeStruct((dests, LANES, width), BF16),
            jax.ShapeDtypeStruct((dests, 16, width), F32),
            jax.ShapeDtypeStruct(filter_inverse.shape, F32),
        ],
        compiler_params=small,
        cost_estimate=pl.CostEstimate(flops=4 * 10**9, bytes_accessed=2**21, transcendentals=0),
        name="prepare",
    )(recv_cell, filter_inverse, energies)
    outgoing = pl.pallas_call(
        functools.partial(send_kernel, float(elements * slabs)),
        in_specs=[smem, smem] + [whole] * 4,
        out_specs=whole,
        out_shape=jax.ShapeDtypeStruct((4 * dests, 8, LANES), F32),
        compiler_params=small,
        name="send",
    )(place, send_count.reshape(-1), parts, energies, rho, picks)
    peers = [[i * slabs + j for i in range(c, groups, 2) for j in range(slabs)] for c in range(2)]
    got = lax.all_to_all(
        outgoing, ("sample", "space"), split_axis=0, concat_axis=0, tiled=True, axis_index_groups=peers
    )
    compliance, sens, energy = pl.pallas_call(
        owner_kernel,
        in_specs=[whole] * 4,
        out_specs=[whole] * 3,
        out_shape=[jax.ShapeDtypeStruct((1, 64), F32)] + [jax.ShapeDtypeStruct((1, 1, sub_rows), F32)] * 2,
        compiler_params=small,
        name="owner",
    )(got, cell_hot, cell_mine, near_filter)
    return (compliance.reshape(-1), sens, energy)


def solution(mesh):
    in_specs = (
        P("sample", None, "space"),
        P(None, "space"),
        P("space"),
        P(),
        P(),
        P("space", None, None, None),
        P("space", None, None),
        P("sample", "space", None, None),
    )
    out_specs = (P(), P("sample", "space", None), P("sample", "space", None))
    return jax.shard_map(body, mesh=mesh, in_specs=in_specs, out_specs=out_specs, check_vma=False)
```

```python
import functools

import jax
import jax.numpy as jnp
from jax import lax
from jax.experimental import pallas as pl
from jax.experimental.pallas import tpu as pltpu
from jax.sharding import PartitionSpec as P

penalty = 3.0
spread_weight = 0.5
epsilon = 1e-06

LANES = 128
BLOCK = 2048
FILL = 29
UNROLL = 128
ROWS = 16
F32 = jnp.float32
BF16 = jnp.bfloat16


def energy_kernel(place_ref, links_ref, own_ref, other_ref, weight_ref, density_ref, out_ref, parts_ref, table, rows, *rest):
    links, sem = rest[:8], rest[8]
    elements = links_ref.shape[0] // 8

    def link_copy(c, q):
        start = pl.multiple_of(c * elements + place_ref[q] * BLOCK, BLOCK)
        there = links[c].at[pl.ds(pl.multiple_of(q * BLOCK, BLOCK), BLOCK)]
        return pltpu.make_async_copy(links_ref.at[pl.ds(start, BLOCK)], there, sem.at[c, q])

    for q in range(4):
        for c in range(8):
            link_copy(c, q).start()

    row = lax.broadcasted_iota(jnp.int32, (LANES // 2, LANES), 0)
    lane = lax.broadcasted_iota(jnp.int32, (LANES // 2, LANES), 1)
    twice = jnp.where(row == lane % (LANES // 2), 1.0, 0.0).astype(BF16)

    def fill(n, _):
        at = pl.ds(pl.multiple_of(n * (FILL * LANES), LANES), FILL * LANES)
        own, other = own_ref[:, at], other_ref[:, at]
        half = []
        for k in range(3):
            half += [own[8 * k : 8 * k + 8], other[8 * k : 8 * k + 8]]
        half = jnp.concatenate(half + [jnp.zeros((ROWS, FILL * LANES), F32)], axis=0).astype(BF16)
        table[at, :] = lax.dot_general(half, twice, (((0,), (0,)), ((), ())), preferred_element_type=F32)
        return 0

    lax.fori_loop(0, table.shape[0] // (FILL * LANES), fill, 0)

    first_half = lax.broadcasted_iota(jnp.int32, (1, LANES), 1) < LANES // 2
    reach = 4 * BLOCK - UNROLL + 1

    def group(q, acc):
        for c in range(8):
            link_copy(c, q).wait()

        def gather(t, _):
            start = pl.multiple_of(t * UNROLL, UNROLL)
            view = rows.at[pl.ds(start, UNROLL)]
            e = q * BLOCK + start
            for u in range(UNROLL):
                for p in range(4):
                    low = table[pl.ds(links[2 * p].at[pl.ds(u, reach)][e], 1), :]
                    high = table[pl.ds(links[2 * p + 1].at[pl.ds(u, reach)][e], 1), :]
                    view[u : u + 1, p * LANES : (p + 1) * LANES] = jnp.where(first_half, low, high)
            return 0

        lax.fori_loop(0, BLOCK // UNROLL, gather, 0)
        field = rows[...]
        applied = jnp.dot(field.astype(BF16), weight_ref[...], preferred_element_type=F32)
        product = field * applied
        folded = product[:, :LANES]
        for p in range(1, 4):
            folded = folded + product[:, p * LANES : (p + 1) * LANES]
        turned = folded.T
        half = turned[: LANES // 2] + turned[LANES // 2 :]
        energy = half[:ROWS] + half[ROWS : 2 * ROWS] + half[2 * ROWS : 3 * ROWS]
        out_ref[q] = energy
        rho = density_ref[place_ref[q]]
        scaled = energy * (rho * rho * rho)
        for p in range(BLOCK // LANES):
            acc = acc + scaled[:, p * LANES : (p + 1) * LANES]
        return acc

    acc = lax.fori_loop(0, 4, group, jnp.zeros((ROWS, LANES), F32))
    column = jnp.sum(acc, axis=1, keepdims=True)
    row_id = lax.broadcasted_iota(jnp.int32, (ROWS, 64), 0)
    lane = lax.broadcasted_iota(jnp.int32, (ROWS, 64), 1)
    spot = jnp.where(row_id < 8, place_ref[4] * 8 + row_id, place_ref[5] * 8 + row_id - 8)
    row = jnp.sum(jnp.where(lane == spot, column, 0.0), axis=0, keepdims=True)
    parts_ref[...] = jnp.broadcast_to(row, parts_ref.shape)


def split(x):
    high = x.astype(BF16)
    return high, (x - high.astype(F32)).astype(BF16)


def prepare_kernel(cells_ref, filter_in, _, hot_ref, mine_ref, filter_ref):
    high, low = split(filter_in[...])
    filter_ref[...] = jnp.concatenate([high, low, high], axis=1)
    sources, width = cells_ref.shape[2:]
    low_id = lax.broadcasted_iota(jnp.int32, (LANES, width), 0)
    high_id = lax.broadcasted_iota(jnp.int32, (16, width), 0)
    for j in range(sources):
        cell = cells_ref[0, 0, j : j + 1, :]
        at = slice(j * width, (j + 1) * width)
        hot_ref[:, at] = jnp.where(low_id == (cell & (LANES - 1)), 1.0, 0.0).astype(BF16)
        mine_ref[:, at] = jnp.where(high_id == (cell >> 7), 1.0, 0.0)


def send_kernel(elements, place_ref, count_ref, parts_ref, energy_ref, density_ref, picks_ref, out_ref):
    comp = jnp.sum(parts_ref[...], axis=0, keepdims=True) / elements
    lane = lax.broadcasted_iota(jnp.int32, (1, 64), 1)
    near = jnp.sum(comp, axis=1, keepdims=True) / ROWS
    away = jnp.where((lane >> 4) == (place_ref[4] >> 1), comp - near, 0.0)
    scale = jnp.max(jnp.abs(away), axis=1, keepdims=True)
    away = away / jnp.maximum(scale, 1e-30)
    row_id = lax.broadcasted_iota(jnp.int32, (ROWS, 64), 0)
    lanes = lax.broadcasted_iota(jnp.int32, (ROWS, 64), 1)
    spot = jnp.where(row_id < 8, place_ref[4] * 8 + row_id, place_ref[5] * 8 + row_id - 8)
    column = jnp.sum(jnp.where(lanes == spot, away, 0.0), axis=1, keepdims=True)
    comp = jnp.concatenate([comp, jnp.zeros_like(comp)], axis=1)
    wide = lax.broadcasted_iota(jnp.int32, (1, LANES), 1)
    facts = jnp.concatenate([comp, jnp.where(wide < 64, near, scale)], axis=0)
    _, dests, width = picks_ref.shape
    low_id = lax.broadcasted_iota(jnp.int32, (LANES, width), 0).astype(jnp.int16)
    one, zero = jnp.ones((LANES, width), BF16), jnp.zeros((LANES, width), BF16)
    high_id = lax.broadcasted_iota(jnp.int32, (16, width), 0)
    slot = lax.broadcasted_iota(jnp.int32, (16, width), 1)
    for q in range(4):
        energy = energy_ref[q]
        rho = density_ref[place_ref[q]]
        total = jnp.sum(energy, axis=0, keepdims=True) / 64.0
        tilted = jnp.sum(column * energy, axis=0, keepdims=True) / 64.0
        slope = -penalty * rho * rho
        both = [f[:, h * LANES : (h + 1) * LANES] for f in (slope * total, slope * tilted, total) for h in range(16)]
        table = jnp.concatenate(split(jnp.concatenate(both, axis=0)), axis=0)
        for d in range(dests):
            pick = picks_ref[q, d : d + 1, :]
            hot = jnp.where(low_id == (pick & (LANES - 1)).astype(jnp.int16), one, zero)
            found = jnp.dot(table, hot, preferred_element_type=F32)
            found = found[:48] + found[48:]
            live = (high_id == (pick >> 7)) & (slot < count_ref[place_ref[q] * 16 + d])
            for f in range(3):
                got = jnp.sum(jnp.where(live, found[16 * f : 16 * f + 16], 0.0), axis=0, keepdims=True)
                for p in range(width // LANES):
                    r = f * (width // LANES) + p
                    out_ref[q * dests + d, r : r + 1, :] = got[:, p * LANES : (p + 1) * LANES]
            out_ref[q * dests + d, 6:8, :] = facts


def owner_kernel(got_ref, hot_ref, mine_ref, filter_ref, comp_ref, sens_ref, energy_ref):
    sources = got_ref.shape[0] // 4
    facts = [got_ref[q * sources, 6:8, :] for q in range(4)]
    comp = (facts[0] + facts[1] + facts[2] + facts[3])[:1, :64]
    comp_ref[...] = comp
    center = jnp.mean(comp, axis=1, keepdims=True)
    spread = jnp.sqrt(jnp.mean((comp - center) ** 2, axis=1, keepdims=True) + epsilon)
    row_id = lax.broadcasted_iota(jnp.int32, (8, LANES), 0)
    factors = []
    for q in range(4):
        near, scale = facts[q][1:2, :1], facts[q][1:2, 64:65]
        plain = 1.0 + spread_weight * (near - center) / spread
        factors.append(jnp.where(row_id < 2, plain, jnp.where(row_id < 4, spread_weight * (scale / spread), 1.0)))
    sens, energy = [], []
    for j in range(sources):
        share = factors[0] * got_ref[j]
        for q in range(1, 4):
            share = share + factors[q] * got_ref[q * sources + j]
        value = share[0:2] + share[2:4]
        sens += [value[0:1], value[1:2]]
        energy += [share[4:5], share[5:6]]
    mine = mine_ref[...]
    rows = jnp.concatenate([mine * jnp.concatenate(field, axis=1) for field in (sens, energy)], axis=0)
    rows = jnp.concatenate(split(rows), axis=0)
    node = lax.dot_general(rows, hot_ref[...], (((1,), (1,)), ((), ())), preferred_element_type=F32)
    node = node[:32] + node[32:]
    high, low = split(node)
    result = lax.dot_general(
        jnp.concatenate([high, high, low], axis=1), filter_ref[...], (((1,), (1,)), ((), ())),
        preferred_element_type=F32,
    )
    for p in range(16):
        sens_ref[0, :, p * LANES : (p + 1) * LANES] = result[p : p + 1]
        energy_ref[0, :, p * LANES : (p + 1) * LANES] = result[16 + p : 17 + p]


def block_stiffness(stiffness):
    lane = jnp.arange(512, dtype=jnp.int32)
    spot = lane % 64
    corner = 2 * (lane // LANES) + (lane % LANES) // 64
    dof = jnp.where(spot < 48, 8 * (spot // ROWS) + corner, -1)
    hot = (dof[:, None] == jnp.arange(24, dtype=jnp.int32)[None, :]).astype(BF16)
    wide = jnp.dot(hot, jnp.dot(stiffness.T, hot.T, preferred_element_type=F32).astype(BF16), preferred_element_type=F32)
    same = (lane % ROWS)[:, None] == (lane % ROWS)[None, :]
    return jnp.where(same, wide, 0.0).astype(BF16)


def body(displacements, connectivity, density, stiffness, filter_inverse, send_rows, send_count, recv_cell):
    group_id = lax.axis_index("sample")
    core = group_id % 2
    node_count = displacements.shape[2]
    elements = density.shape[0]
    groups = 8
    sub_rows = elements // groups
    slabs = lax.axis_size("space")
    nodes = (node_count + LANES - 1) // LANES * LANES

    own = jnp.transpose(displacements, (1, 0, 2)).reshape(24, node_count).astype(F32)
    own = jnp.pad(own, ((0, 0), (0, nodes - node_count)))
    other = lax.ppermute(own, "sample", [(i, i ^ 1) for i in range(8)])
    links = connectivity.reshape(-1)
    rho = density.reshape(groups, 1, sub_rows)
    weights = block_stiffness(stiffness)

    place = jnp.stack([2 * q + core for q in range(4)] + [group_id, group_id ^ 1]).astype(jnp.int32)
    whole = pl.BlockSpec(memory_space=pltpu.VMEM)
    smem = pl.BlockSpec(memory_space=pltpu.SMEM)
    energies, mine = pl.pallas_call(
        energy_kernel,
        in_specs=[smem, pl.BlockSpec(memory_space=pl.ANY)] + [whole] * 4,
        out_specs=[whole] * 2,
        out_shape=[jax.ShapeDtypeStruct((4, ROWS, sub_rows), F32), jax.ShapeDtypeStruct((2 * slabs, 64), F32)],
        scratch_shapes=[pltpu.VMEM((nodes, LANES), F32), pltpu.VMEM((BLOCK, 4 * LANES), F32)]
        + [pltpu.SMEM((4 * BLOCK,), jnp.int32)] * 8
        + [pltpu.SemaphoreType.DMA((8, 4))],
        compiler_params=pltpu.CompilerParams(vmem_limit_bytes=30 * 2**20),
        name="energy",
    )(place, links, own, other, weights, rho)
    chips = [[i * slabs + j for i in (c, c + 1) for j in range(slabs)] for c in range(0, groups, 2)]
    parts = lax.all_to_all(mine, ("sample", "space"), split_axis=0, concat_axis=0, tiled=True, axis_index_groups=chips)
    dests, width = send_rows.shape[-2:]
    picks = lax.dynamic_index_in_dim(send_rows.reshape(4, 2, dests, width), core, 1, keepdims=False)
    small = pltpu.CompilerParams(vmem_limit_bytes=8 * 2**20)
    cell_hot, cell_mine, near_filter = pl.pallas_call(
        prepare_kernel,
        in_specs=[whole, whole, pl.BlockSpec(memory_space=pl.ANY)],
        out_specs=[whole] * 3,
        out_shape=[
            jax.ShapeDtypeStruct((LANES, dests * width), BF16),
            jax.ShapeDtypeStruct((16, dests * width), F32),
            jax.ShapeDtypeStruct((LANES, 3 * LANES), BF16),
        ],
        compiler_params=small,
        cost_estimate=pl.CostEstimate(flops=4 * 10**9, bytes_accessed=2**21, transcendentals=0),
        name="prepare",
    )(recv_cell, filter_inverse, energies)
    outgoing = pl.pallas_call(
        functools.partial(send_kernel, float(elements * slabs)),
        in_specs=[smem, smem] + [whole] * 4,
        out_specs=whole,
        out_shape=jax.ShapeDtypeStruct((4 * dests, 8, LANES), F32),
        compiler_params=small,
        name="send",
    )(place, send_count.reshape(-1), parts, energies, rho, picks)
    peers = [[i * slabs + j for i in range(c, groups, 2) for j in range(slabs)] for c in range(2)]
    got = lax.all_to_all(
        outgoing, ("sample", "space"), split_axis=0, concat_axis=0, tiled=True, axis_index_groups=peers
    )
    compliance, sens, energy = pl.pallas_call(
        owner_kernel,
        in_specs=[whole] * 4,
        out_specs=[whole] * 3,
        out_shape=[jax.ShapeDtypeStruct((1, 64), F32)] + [jax.ShapeDtypeStruct((1, 1, sub_rows), F32)] * 2,
        compiler_params=small,
        name="owner",
    )(got, cell_hot, cell_mine, near_filter)
    return (compliance.reshape(-1), sens, energy)


def solution(mesh):
    in_specs = (
        P("sample", None, "space"),
        P(None, "space"),
        P("space"),
        P(),
        P(),
        P("space", None, None, None),
        P("space", None, None),
        P("sample", "space", None, None),
    )
    out_specs = (P(), P("sample", "space", None), P("sample", "space", None))
    return jax.shard_map(body, mesh=mesh, in_specs=in_specs, out_specs=out_specs, check_vma=False)
```

```python
import functools

import jax
import jax.numpy as jnp
from jax import lax
from jax.experimental import pallas as pl
from jax.experimental.pallas import tpu as pltpu
from jax.sharding import PartitionSpec as P

penalty = 3.0
spread_weight = 0.5
epsilon = 1e-06

LANES = 128
BLOCK = 2048
FILL = 29
UNROLL = 256
ROWS = 16
F32 = jnp.float32
BF16 = jnp.bfloat16


def energy_kernel(place_ref, links_ref, own_ref, other_ref, weight_ref, density_ref, out_ref, parts_ref, table, rows, *rest):
    links, sem = rest[:8], rest[8]
    elements = links_ref.shape[0] // 8

    def link_copy(c, q):
        start = pl.multiple_of(c * elements + place_ref[q] * BLOCK, BLOCK)
        there = links[c].at[pl.ds(pl.multiple_of(q * BLOCK, BLOCK), BLOCK)]
        return pltpu.make_async_copy(links_ref.at[pl.ds(start, BLOCK)], there, sem.at[c, q])

    for q in range(4):
        for c in range(8):
            link_copy(c, q).start()

    row = lax.broadcasted_iota(jnp.int32, (LANES // 2, LANES), 0)
    lane = lax.broadcasted_iota(jnp.int32, (LANES // 2, LANES), 1)
    twice = jnp.where(row == lane % (LANES // 2), 1.0, 0.0).astype(BF16)

    def fill(n, _):
        at = pl.ds(pl.multiple_of(n * (FILL * LANES), LANES), FILL * LANES)
        own, other = own_ref[:, at], other_ref[:, at]
        half = []
        for k in range(3):
            half += [own[8 * k : 8 * k + 8], other[8 * k : 8 * k + 8]]
        half = jnp.concatenate(half + [jnp.zeros((ROWS, FILL * LANES), F32)], axis=0).astype(BF16)
        table[at, :] = lax.dot_general(half, twice, (((0,), (0,)), ((), ())), preferred_element_type=F32)
        return 0

    lax.fori_loop(0, table.shape[0] // (FILL * LANES), fill, 0)

    first_half = lax.broadcasted_iota(jnp.int32, (1, LANES), 1) < LANES // 2
    reach = 4 * BLOCK - UNROLL + 1

    def group(q, acc):
        for c in range(8):
            link_copy(c, q).wait()

        def gather(t, _):
            start = pl.multiple_of(t * UNROLL, UNROLL)
            view = rows.at[pl.ds(start, UNROLL)]
            e = q * BLOCK + start
            for u in range(UNROLL):
                for p in range(4):
                    low = table[pl.ds(links[2 * p].at[pl.ds(u, reach)][e], 1), :]
                    high = table[pl.ds(links[2 * p + 1].at[pl.ds(u, reach)][e], 1), :]
                    view[u : u + 1, p * LANES : (p + 1) * LANES] = jnp.where(first_half, low, high)
            return 0

        lax.fori_loop(0, BLOCK // UNROLL, gather, 0)
        field = rows[...]
        applied = jnp.dot(field.astype(BF16), weight_ref[...], preferred_element_type=F32)
        product = field * applied
        folded = product[:, :LANES]
        for p in range(1, 4):
            folded = folded + product[:, p * LANES : (p + 1) * LANES]
        turned = folded.T
        half = turned[: LANES // 2] + turned[LANES // 2 :]
        energy = half[:ROWS] + half[ROWS : 2 * ROWS] + half[2 * ROWS : 3 * ROWS]
        out_ref[q] = energy
        rho = density_ref[place_ref[q]]
        scaled = energy * (rho * rho * rho)
        for p in range(BLOCK // LANES):
            acc = acc + scaled[:, p * LANES : (p + 1) * LANES]
        return acc

    acc = lax.fori_loop(0, 4, group, jnp.zeros((ROWS, LANES), F32))
    column = jnp.sum(acc, axis=1, keepdims=True)
    row_id = lax.broadcasted_iota(jnp.int32, (ROWS, 64), 0)
    lane = lax.broadcasted_iota(jnp.int32, (ROWS, 64), 1)
    spot = jnp.where(row_id < 8, place_ref[4] * 8 + row_id, place_ref[5] * 8 + row_id - 8)
    row = jnp.sum(jnp.where(lane == spot, column, 0.0), axis=0, keepdims=True)
    parts_ref[...] = jnp.broadcast_to(row, parts_ref.shape)


def split(x):
    high = x.astype(BF16)
    return high, (x - high.astype(F32)).astype(BF16)


def prepare_kernel(cells_ref, filter_in, _, hot_ref, mine_ref, filter_ref):
    high, low = split(filter_in[...])
    filter_ref[...] = jnp.concatenate([high, low, high], axis=1)
    sources, width = cells_ref.shape[2:]
    low_id = lax.broadcasted_iota(jnp.int32, (LANES, width), 0)
    high_id = lax.broadcasted_iota(jnp.int32, (16, width), 0)
    for j in range(sources):
        cell = cells_ref[0, 0, j : j + 1, :]
        at = slice(j * width, (j + 1) * width)
        hot_ref[:, at] = jnp.where(low_id == (cell & (LANES - 1)), 1.0, 0.0).astype(BF16)
        mine_ref[:, at] = jnp.where(high_id == (cell >> 7), 1.0, 0.0)


def send_kernel(elements, place_ref, count_ref, parts_ref, energy_ref, density_ref, picks_ref, out_ref):
    comp = jnp.sum(parts_ref[...], axis=0, keepdims=True) / elements
    lane = lax.broadcasted_iota(jnp.int32, (1, 64), 1)
    near = jnp.sum(comp, axis=1, keepdims=True) / ROWS
    away = jnp.where((lane >> 4) == (place_ref[4] >> 1), comp - near, 0.0)
    scale = jnp.max(jnp.abs(away), axis=1, keepdims=True)
    away = away / jnp.maximum(scale, 1e-30)
    row_id = lax.broadcasted_iota(jnp.int32, (ROWS, 64), 0)
    lanes = lax.broadcasted_iota(jnp.int32, (ROWS, 64), 1)
    spot = jnp.where(row_id < 8, place_ref[4] * 8 + row_id, place_ref[5] * 8 + row_id - 8)
    column = jnp.sum(jnp.where(lanes == spot, away, 0.0), axis=1, keepdims=True)
    comp = jnp.concatenate([comp, jnp.zeros_like(comp)], axis=1)
    wide = lax.broadcasted_iota(jnp.int32, (1, LANES), 1)
    facts = jnp.concatenate([comp, jnp.where(wide < 64, near, scale)], axis=0)
    _, dests, width = picks_ref.shape
    low_id = lax.broadcasted_iota(jnp.int32, (LANES, width), 0).astype(jnp.int16)
    one, zero = jnp.ones((LANES, width), BF16), jnp.zeros((LANES, width), BF16)
    high_id = lax.broadcasted_iota(jnp.int32, (16, width), 0)
    slot = lax.broadcasted_iota(jnp.int32, (16, width), 1)
    for q in range(4):
        energy = energy_ref[q]
        rho = density_ref[place_ref[q]]
        total = jnp.sum(energy, axis=0, keepdims=True) / 64.0
        tilted = jnp.sum(column * energy, axis=0, keepdims=True) / 64.0
        slope = -penalty * rho * rho
        both = [f.reshape(16, LANES) for f in (slope * total, slope * tilted, total)]
        table = jnp.concatenate(split(jnp.concatenate(both, axis=0)), axis=0)
        for d in range(dests):
            pick = picks_ref[q, d : d + 1, :]
            hot = jnp.where(low_id == (pick & (LANES - 1)).astype(jnp.int16), one, zero)
            found = jnp.dot(table, hot, preferred_element_type=F32)
            found = found[:48] + found[48:]
            live = (high_id == (pick >> 7)) & (slot < count_ref[place_ref[q] * 16 + d])
            for f in range(3):
                got = jnp.sum(jnp.where(live, found[16 * f : 16 * f + 16], 0.0), axis=0, keepdims=True)
                for p in range(width // LANES):
                    r = f * (width // LANES) + p
                    out_ref[q * dests + d, r : r + 1, :] = got[:, p * LANES : (p + 1) * LANES]
            out_ref[q * dests + d, 6:8, :] = facts


def owner_kernel(got_ref, hot_ref, mine_ref, filter_ref, comp_ref, sens_ref, energy_ref):
    sources = got_ref.shape[0] // 4
    facts = [got_ref[q * sources, 6:8, :] for q in range(4)]
    comp = (facts[0] + facts[1] + facts[2] + facts[3])[:1, :64]
    comp_ref[...] = comp
    center = jnp.mean(comp, axis=1, keepdims=True)
    spread = jnp.sqrt(jnp.mean((comp - center) ** 2, axis=1, keepdims=True) + epsilon)
    row_id = lax.broadcasted_iota(jnp.int32, (8, LANES), 0)
    factors = []
    for q in range(4):
        near, scale = facts[q][1:2, :1], facts[q][1:2, 64:65]
        plain = 1.0 + spread_weight * (near - center) / spread
        factors.append(jnp.where(row_id < 2, plain, jnp.where(row_id < 4, spread_weight * (scale / spread), 1.0)))
    sens, energy = [], []
    for j in range(sources):
        share = factors[0] * got_ref[j]
        for q in range(1, 4):
            share = share + factors[q] * got_ref[q * sources + j]
        value = share[0:2] + share[2:4]
        sens += [value[0:1], value[1:2]]
        energy += [share[4:5], share[5:6]]
    mine = mine_ref[...]
    rows = jnp.concatenate([mine * jnp.concatenate(field, axis=1) for field in (sens, energy)], axis=0)
    rows = jnp.concatenate(split(rows), axis=0)
    node = lax.dot_general(rows, hot_ref[...], (((1,), (1,)), ((), ())), preferred_element_type=F32)
    node = node[:32] + node[32:]
    high, low = split(node)
    result = lax.dot_general(
        jnp.concatenate([high, high, low], axis=1), filter_ref[...], (((1,), (1,)), ((), ())),
        preferred_element_type=F32,
    )
    for p in range(16):
        sens_ref[0, :, p * LANES : (p + 1) * LANES] = result[p : p + 1]
        energy_ref[0, :, p * LANES : (p + 1) * LANES] = result[16 + p : 17 + p]


def block_stiffness(stiffness):
    lane = jnp.arange(512, dtype=jnp.int32)
    spot = lane % 64
    corner = 2 * (lane // LANES) + (lane % LANES) // 64
    dof = jnp.where(spot < 48, 8 * (spot // ROWS) + corner, -1)
    hot = (dof[:, None] == jnp.arange(24, dtype=jnp.int32)[None, :]).astype(BF16)
    wide = jnp.dot(hot, jnp.dot(stiffness.T, hot.T, preferred_element_type=F32).astype(BF16), preferred_element_type=F32)
    same = (lane % ROWS)[:, None] == (lane % ROWS)[None, :]
    return jnp.where(same, wide, 0.0).astype(BF16)


def body(displacements, connectivity, density, stiffness, filter_inverse, send_rows, send_count, recv_cell):
    group_id = lax.axis_index("sample")
    core = group_id % 2
    node_count = displacements.shape[2]
    elements = density.shape[0]
    groups = 8
    sub_rows = elements // groups
    slabs = lax.axis_size("space")
    nodes = (node_count + LANES - 1) // LANES * LANES

    own = jnp.transpose(displacements, (1, 0, 2)).reshape(24, node_count).astype(F32)
    own = jnp.pad(own, ((0, 0), (0, nodes - node_count)))
    other = lax.ppermute(own, "sample", [(i, i ^ 1) for i in range(8)])
    links = connectivity.reshape(-1)
    rho = density.reshape(groups, 1, sub_rows)
    weights = block_stiffness(stiffness)

    place = jnp.stack([2 * q + core for q in range(4)] + [group_id, group_id ^ 1]).astype(jnp.int32)
    whole = pl.BlockSpec(memory_space=pltpu.VMEM)
    smem = pl.BlockSpec(memory_space=pltpu.SMEM)
    energies, mine = pl.pallas_call(
        energy_kernel,
        in_specs=[smem, pl.BlockSpec(memory_space=pl.ANY)] + [whole] * 4,
        out_specs=[whole] * 2,
        out_shape=[jax.ShapeDtypeStruct((4, ROWS, sub_rows), F32), jax.ShapeDtypeStruct((2 * slabs, 64), F32)],
        scratch_shapes=[pltpu.VMEM((nodes, LANES), F32), pltpu.VMEM((BLOCK, 4 * LANES), F32)]
        + [pltpu.SMEM((4 * BLOCK,), jnp.int32)] * 8
        + [pltpu.SemaphoreType.DMA((8, 4))],
        compiler_params=pltpu.CompilerParams(vmem_limit_bytes=30 * 2**20),
        name="energy",
    )(place, links, own, other, weights, rho)
    chips = [[i * slabs + j for i in (c, c + 1) for j in range(slabs)] for c in range(0, groups, 2)]
    parts = lax.all_to_all(mine, ("sample", "space"), split_axis=0, concat_axis=0, tiled=True, axis_index_groups=chips)
    dests, width = send_rows.shape[-2:]
    picks = lax.dynamic_index_in_dim(send_rows.reshape(4, 2, dests, width), core, 1, keepdims=False)
    small = pltpu.CompilerParams(vmem_limit_bytes=8 * 2**20)
    cell_hot, cell_mine, near_filter = pl.pallas_call(
        prepare_kernel,
        in_specs=[whole, whole, pl.BlockSpec(memory_space=pl.ANY)],
        out_specs=[whole] * 3,
        out_shape=[
            jax.ShapeDtypeStruct((LANES, dests * width), BF16),
            jax.ShapeDtypeStruct((16, dests * width), F32),
            jax.ShapeDtypeStruct((LANES, 3 * LANES), BF16),
        ],
        compiler_params=small,
        cost_estimate=pl.CostEstimate(flops=4 * 10**9, bytes_accessed=2**21, transcendentals=0),
        name="prepare",
    )(recv_cell, filter_inverse, energies)
    outgoing = pl.pallas_call(
        functools.partial(send_kernel, float(elements * slabs)),
        in_specs=[smem, smem] + [whole] * 4,
        out_specs=whole,
        out_shape=jax.ShapeDtypeStruct((4 * dests, 8, LANES), F32),
        compiler_params=small,
        name="send",
    )(place, send_count.reshape(-1), parts, energies, rho, picks)
    peers = [[i * slabs + j for i in range(c, groups, 2) for j in range(slabs)] for c in range(2)]
    got = lax.all_to_all(
        outgoing, ("sample", "space"), split_axis=0, concat_axis=0, tiled=True, axis_index_groups=peers
    )
    compliance, sens, energy = pl.pallas_call(
        owner_kernel,
        in_specs=[whole] * 4,
        out_specs=[whole] * 3,
        out_shape=[jax.ShapeDtypeStruct((1, 64), F32)] + [jax.ShapeDtypeStruct((1, 1, sub_rows), F32)] * 2,
        compiler_params=small,
        name="owner",
    )(got, cell_hot, cell_mine, near_filter)
    return (compliance.reshape(-1), sens, energy)


def solution(mesh):
    in_specs = (
        P("sample", None, "space"),
        P(None, "space"),
        P("space"),
        P(),
        P(),
        P("space", None, None, None),
        P("space", None, None),
        P("sample", "space", None, None),
    )
    out_specs = (P(), P("sample", "space", None), P("sample", "space", None))
    return jax.shard_map(body, mesh=mesh, in_specs=in_specs, out_specs=out_specs, check_vma=False)
```

```python
import functools

import jax
import jax.numpy as jnp
from jax import lax
from jax.experimental import pallas as pl
from jax.experimental.pallas import tpu as pltpu
from jax.sharding import PartitionSpec as P

penalty = 3.0
spread_weight = 0.5
epsilon = 1e-06

LANES = 128
BLOCK = 2048
FILL = 29
UNROLL = 256
ROWS = 16
F32 = jnp.float32
BF16 = jnp.bfloat16


def energy_kernel(place_ref, links_ref, own_ref, other_ref, weight_ref, density_ref, out_ref, parts_ref, table, rows, *rest):
    links, sem = rest[:8], rest[8]
    elements = links_ref.shape[0] // 8

    def link_copy(c, q):
        start = pl.multiple_of(c * elements + place_ref[q] * BLOCK, BLOCK)
        there = links[c].at[pl.ds(pl.multiple_of(q * BLOCK, BLOCK), BLOCK)]
        return pltpu.make_async_copy(links_ref.at[pl.ds(start, BLOCK)], there, sem.at[c, q])

    for q in range(4):
        for c in range(8):
            link_copy(c, q).start()

    row = lax.broadcasted_iota(jnp.int32, (LANES // 2, LANES), 0)
    lane = lax.broadcasted_iota(jnp.int32, (LANES // 2, LANES), 1)
    twice = jnp.where(row == lane % (LANES // 2), 1.0, 0.0).astype(BF16)

    def fill(n, _):
        at = pl.ds(pl.multiple_of(n * (FILL * LANES), LANES), FILL * LANES)
        own, other = own_ref[:, at], other_ref[:, at]
        half = []
        for k in range(3):
            half += [own[8 * k : 8 * k + 8], other[8 * k : 8 * k + 8]]
        half = jnp.concatenate(half + [jnp.zeros((ROWS, FILL * LANES), F32)], axis=0).astype(BF16)
        table[at, :] = lax.dot_general(half, twice, (((0,), (0,)), ((), ())), preferred_element_type=F32)
        return 0

    lax.fori_loop(0, table.shape[0] // (FILL * LANES), fill, 0)

    first_half = lax.broadcasted_iota(jnp.int32, (1, LANES), 1) < LANES // 2
    reach = 4 * BLOCK - UNROLL + 1

    def group(q, acc):
        for c in range(8):
            link_copy(c, q).wait()

        def gather(t, _):
            start = pl.multiple_of(t * UNROLL, UNROLL)
            view = rows.at[pl.ds(start, UNROLL)]
            e = q * BLOCK + start
            for u in range(UNROLL):
                for p in range(4):
                    low = table[pl.ds(links[2 * p].at[pl.ds(u, reach)][e], 1), :]
                    high = table[pl.ds(links[2 * p + 1].at[pl.ds(u, reach)][e], 1), :]
                    view[u : u + 1, p * LANES : (p + 1) * LANES] = jnp.where(first_half, low, high)
            return 0

        lax.fori_loop(0, BLOCK // UNROLL, gather, 0)
        field = rows[...]
        applied = jnp.dot(field.astype(BF16), weight_ref[...], preferred_element_type=F32)
        product = field * applied
        folded = product[:, :LANES]
        for p in range(1, 4):
            folded = folded + product[:, p * LANES : (p + 1) * LANES]
        turned = folded.T
        half = turned[: LANES // 2] + turned[LANES // 2 :]
        energy = half[:ROWS] + half[ROWS : 2 * ROWS] + half[2 * ROWS : 3 * ROWS]
        out_ref[q] = energy
        rho = density_ref[place_ref[q]]
        scaled = energy * (rho * rho * rho)
        for p in range(BLOCK // LANES):
            acc = acc + scaled[:, p * LANES : (p + 1) * LANES]
        return acc

    acc = lax.fori_loop(0, 4, group, jnp.zeros((ROWS, LANES), F32))
    column = jnp.sum(acc, axis=1, keepdims=True)
    row_id = lax.broadcasted_iota(jnp.int32, (ROWS, 64), 0)
    lane = lax.broadcasted_iota(jnp.int32, (ROWS, 64), 1)
    spot = jnp.where(row_id < 8, place_ref[4] * 8 + row_id, place_ref[5] * 8 + row_id - 8)
    row = jnp.sum(jnp.where(lane == spot, column, 0.0), axis=0, keepdims=True)
    parts_ref[...] = jnp.broadcast_to(row, parts_ref.shape)


def split(x):
    high = x.astype(BF16)
    return high, (x - high.astype(F32)).astype(BF16)


def prepare_kernel(cells_ref, filter_in, _, hot_ref, mine_ref, filter_ref):
    high, low = split(filter_in[...])
    filter_ref[...] = jnp.concatenate([high, low, high], axis=1)
    sources, width = cells_ref.shape[2:]
    low_id = lax.broadcasted_iota(jnp.int32, (LANES, width), 0)
    high_id = lax.broadcasted_iota(jnp.int32, (16, width), 0)
    for j in range(sources):
        cell = cells_ref[0, 0, j : j + 1, :]
        at = slice(j * width, (j + 1) * width)
        hot_ref[:, at] = jnp.where(low_id == (cell & (LANES - 1)), 1.0, 0.0).astype(BF16)
        mine_ref[:, at] = jnp.where(high_id == (cell >> 7), 1.0, 0.0)


def send_kernel(elements, place_ref, count_ref, parts_ref, energy_ref, density_ref, picks_ref, out_hbm, out_ref, sem):
    comp = jnp.sum(parts_ref[...], axis=0, keepdims=True) / elements
    lane = lax.broadcasted_iota(jnp.int32, (1, 64), 1)
    near = jnp.sum(comp, axis=1, keepdims=True) / ROWS
    away = jnp.where((lane >> 4) == (place_ref[4] >> 1), comp - near, 0.0)
    scale = jnp.max(jnp.abs(away), axis=1, keepdims=True)
    away = away / jnp.maximum(scale, 1e-30)
    row_id = lax.broadcasted_iota(jnp.int32, (ROWS, 64), 0)
    lanes = lax.broadcasted_iota(jnp.int32, (ROWS, 64), 1)
    spot = jnp.where(row_id < 8, place_ref[4] * 8 + row_id, place_ref[5] * 8 + row_id - 8)
    column = jnp.sum(jnp.where(lanes == spot, away, 0.0), axis=1, keepdims=True)
    comp = jnp.concatenate([comp, jnp.zeros_like(comp)], axis=1)
    wide = lax.broadcasted_iota(jnp.int32, (1, LANES), 1)
    facts = jnp.concatenate([comp, jnp.where(wide < 64, near, scale)], axis=0)
    _, dests, width = picks_ref.shape
    low_id = lax.broadcasted_iota(jnp.int32, (LANES, width), 0).astype(jnp.int16)
    one, zero = jnp.ones((LANES, width), BF16), jnp.zeros((LANES, width), BF16)
    high_id = lax.broadcasted_iota(jnp.int32, (16, width), 0)
    slot = lax.broadcasted_iota(jnp.int32, (16, width), 1)
    copies = []
    for q in range(4):
        energy = energy_ref[q]
        rho = density_ref[place_ref[q]]
        total = jnp.sum(energy, axis=0, keepdims=True) / 64.0
        tilted = jnp.sum(column * energy, axis=0, keepdims=True) / 64.0
        slope = -penalty * rho * rho
        both = [f.reshape(16, LANES) for f in (slope * total, slope * tilted, total)]
        table = jnp.concatenate(split(jnp.concatenate(both, axis=0)), axis=0)
        for d in range(dests):
            pick = picks_ref[q, d : d + 1, :]
            hot = jnp.where(low_id == (pick & (LANES - 1)).astype(jnp.int16), one, zero)
            found = jnp.dot(table, hot, preferred_element_type=F32)
            found = found[:48] + found[48:]
            live = (high_id == (pick >> 7)) & (slot < count_ref[place_ref[q] * 16 + d])
            for f in range(3):
                got = jnp.sum(jnp.where(live, found[16 * f : 16 * f + 16], 0.0), axis=0, keepdims=True)
                for p in range(width // LANES):
                    r = f * (width // LANES) + p
                    out_ref[q * dests + d, r : r + 1, :] = got[:, p * LANES : (p + 1) * LANES]
            out_ref[q * dests + d, 6:8, :] = facts
        span = pl.ds(q * dests, dests)
        copies.append(pltpu.make_async_copy(out_ref.at[span], out_hbm.at[span], sem.at[q]))
        copies[-1].start()
    for copy in copies:
        copy.wait()


def owner_kernel(got_ref, hot_ref, mine_ref, filter_ref, comp_ref, sens_ref, energy_ref):
    sources = got_ref.shape[0] // 4
    facts = [got_ref[q * sources, 6:8, :] for q in range(4)]
    comp = (facts[0] + facts[1] + facts[2] + facts[3])[:1, :64]
    comp_ref[...] = comp
    center = jnp.mean(comp, axis=1, keepdims=True)
    spread = jnp.sqrt(jnp.mean((comp - center) ** 2, axis=1, keepdims=True) + epsilon)
    row_id = lax.broadcasted_iota(jnp.int32, (8, LANES), 0)
    factors = []
    for q in range(4):
        near, scale = facts[q][1:2, :1], facts[q][1:2, 64:65]
        plain = 1.0 + spread_weight * (near - center) / spread
        factors.append(jnp.where(row_id < 2, plain, jnp.where(row_id < 4, spread_weight * (scale / spread), 1.0)))
    sens, energy = [], []
    for j in range(sources):
        share = factors[0] * got_ref[j]
        for q in range(1, 4):
            share = share + factors[q] * got_ref[q * sources + j]
        value = share[0:2] + share[2:4]
        sens += [value[0:1], value[1:2]]
        energy += [share[4:5], share[5:6]]
    mine = mine_ref[...]
    rows = jnp.concatenate([mine * jnp.concatenate(field, axis=1) for field in (sens, energy)], axis=0)
    rows = jnp.concatenate(split(rows), axis=0)
    node = lax.dot_general(rows, hot_ref[...], (((1,), (1,)), ((), ())), preferred_element_type=F32)
    node = node[:32] + node[32:]
    high, low = split(node)
    result = lax.dot_general(
        jnp.concatenate([high, high, low], axis=1), filter_ref[...], (((1,), (1,)), ((), ())),
        preferred_element_type=F32,
    )
    for p in range(16):
        sens_ref[0, :, p * LANES : (p + 1) * LANES] = result[p : p + 1]
        energy_ref[0, :, p * LANES : (p + 1) * LANES] = result[16 + p : 17 + p]


def block_stiffness(stiffness):
    lane = jnp.arange(512, dtype=jnp.int32)
    spot = lane % 64
    corner = 2 * (lane // LANES) + (lane % LANES) // 64
    dof = jnp.where(spot < 48, 8 * (spot // ROWS) + corner, -1)
    hot = (dof[:, None] == jnp.arange(24, dtype=jnp.int32)[None, :]).astype(BF16)
    wide = jnp.dot(hot, jnp.dot(stiffness.T, hot.T, preferred_element_type=F32).astype(BF16), preferred_element_type=F32)
    same = (lane % ROWS)[:, None] == (lane % ROWS)[None, :]
    return jnp.where(same, wide, 0.0).astype(BF16)


def body(displacements, connectivity, density, stiffness, filter_inverse, send_rows, send_count, recv_cell):
    group_id = lax.axis_index("sample")
    core = group_id % 2
    node_count = displacements.shape[2]
    elements = density.shape[0]
    groups = 8
    sub_rows = elements // groups
    slabs = lax.axis_size("space")
    nodes = (node_count + LANES - 1) // LANES * LANES

    own = jnp.transpose(displacements, (1, 0, 2)).reshape(24, node_count).astype(F32)
    own = jnp.pad(own, ((0, 0), (0, nodes - node_count)))
    other = lax.ppermute(own, "sample", [(i, i ^ 1) for i in range(8)])
    links = connectivity.reshape(-1)
    rho = density.reshape(groups, 1, sub_rows)
    weights = block_stiffness(stiffness)

    place = jnp.stack([2 * q + core for q in range(4)] + [group_id, group_id ^ 1]).astype(jnp.int32)
    whole = pl.BlockSpec(memory_space=pltpu.VMEM)
    smem = pl.BlockSpec(memory_space=pltpu.SMEM)
    energies, mine = pl.pallas_call(
        energy_kernel,
        in_specs=[smem, pl.BlockSpec(memory_space=pl.ANY)] + [whole] * 4,
        out_specs=[whole] * 2,
        out_shape=[jax.ShapeDtypeStruct((4, ROWS, sub_rows), F32), jax.ShapeDtypeStruct((2 * slabs, 64), F32)],
        scratch_shapes=[pltpu.VMEM((nodes, LANES), F32), pltpu.VMEM((BLOCK, 4 * LANES), F32)]
        + [pltpu.SMEM((4 * BLOCK,), jnp.int32)] * 8
        + [pltpu.SemaphoreType.DMA((8, 4))],
        compiler_params=pltpu.CompilerParams(vmem_limit_bytes=30 * 2**20),
        name="energy",
    )(place, links, own, other, weights, rho)
    chips = [[i * slabs + j for i in (c, c + 1) for j in range(slabs)] for c in range(0, groups, 2)]
    parts = lax.all_to_all(mine, ("sample", "space"), split_axis=0, concat_axis=0, tiled=True, axis_index_groups=chips)
    dests, width = send_rows.shape[-2:]
    picks = lax.dynamic_index_in_dim(send_rows.reshape(4, 2, dests, width), core, 1, keepdims=False)
    small = pltpu.CompilerParams(vmem_limit_bytes=8 * 2**20)
    cell_hot, cell_mine, near_filter = pl.pallas_call(
        prepare_kernel,
        in_specs=[whole, whole, pl.BlockSpec(memory_space=pl.ANY)],
        out_specs=[whole] * 3,
        out_shape=[
            jax.ShapeDtypeStruct((LANES, dests * width), BF16),
            jax.ShapeDtypeStruct((16, dests * width), F32),
            jax.ShapeDtypeStruct((LANES, 3 * LANES), BF16),
        ],
        compiler_params=small,
        cost_estimate=pl.CostEstimate(flops=4 * 10**9, bytes_accessed=2**21, transcendentals=0),
        name="prepare",
    )(recv_cell, filter_inverse, energies)
    outgoing = pl.pallas_call(
        functools.partial(send_kernel, float(elements * slabs)),
        in_specs=[smem, smem] + [whole] * 4,
        out_specs=pl.BlockSpec(memory_space=pltpu.HBM),
        out_shape=jax.ShapeDtypeStruct((4 * dests, 8, LANES), F32),
        scratch_shapes=[pltpu.VMEM((4 * dests, 8, LANES), F32), pltpu.SemaphoreType.DMA((4,))],
        compiler_params=small,
        name="send",
    )(place, send_count.reshape(-1), parts, energies, rho, picks)
    peers = [[i * slabs + j for i in range(c, groups, 2) for j in range(slabs)] for c in range(2)]
    got = lax.all_to_all(
        outgoing, ("sample", "space"), split_axis=0, concat_axis=0, tiled=True, axis_index_groups=peers
    )
    compliance, sens, energy = pl.pallas_call(
        owner_kernel,
        in_specs=[whole] * 4,
        out_specs=[whole] * 3,
        out_shape=[jax.ShapeDtypeStruct((1, 64), F32)] + [jax.ShapeDtypeStruct((1, 1, sub_rows), F32)] * 2,
        compiler_params=small,
        name="owner",
    )(got, cell_hot, cell_mine, near_filter)
    return (compliance.reshape(-1), sens, energy)


def solution(mesh):
    in_specs = (
        P("sample", None, "space"),
        P(None, "space"),
        P("space"),
        P(),
        P(),
        P("space", None, None, None),
        P("space", None, None),
        P("sample", "space", None, None),
    )
    out_specs = (P(), P("sample", "space", None), P("sample", "space", None))
    return jax.shard_map(body, mesh=mesh, in_specs=in_specs, out_specs=out_specs, check_vma=False)
```
